256 devices in a mesh: row: 16 (over z, core), col: 16 (over y, x).
Axes of the slice: x: 4, y: 4, z: 8, core: 2. Of those that a mesh axis runs over, the one named last changes fastest.
Arguments:
- inputs: bfloat16 [512, 12288], P('col', 'row'), may hold values from -6 to 6
- first_weight: bfloat16 [12288, 49152], P('row', 'col'), may hold values from -0.0546875 to 0.0546875
- second_weight: bfloat16 [49152, 12288], P('col', 'row'), may hold values from -0.02734375 to 0.02734375
- cotangent: bfloat16 [512, 12288], P('col', 'row'), may hold values from -6 to 6
Outputs:
- output: bfloat16 [512, 12288], P('col', 'row')
- grad_inputs: bfloat16 [512, 12288], P('col', 'row')
The draws below stay inside these ranges and needn't reach their ends.
All inputs are finite; a program needn't handle non-finite values.
Results may differ from the reference program's by a relative error of at most 0.0049.
Values may be sent and summed in bfloat16 or wider, within the bound.
No kernel may reach another device: no remote copies, remote signals or barrier semaphores. Data moves between devices by JAX's collectives and lax.ppermute only.
A program may use at most 128 MiB of HBM per device.

```python
import jax
import jax.numpy as jnp
from jax import lax

D = 12288
FF = 49152
TOKENS = 512


def levels(key, shape, pieces, least, high):
    def one(position, parts):
        heights = jax.random.uniform(jax.random.fold_in(jax.random.fold_in(key, 6), position), (parts,), jnp.float32, least / len(pieces), high / len(pieces))
        return jnp.repeat(jnp.exp(heights), shape[position] // parts).reshape((-1,) + (1,) * (len(shape) - position - 1))

    gain = one(*pieces[0])
    for cut in pieces[1:]:
        gain = gain * one(*cut)
    return gain


def gaussian(key, extent, deviation, most, cuts=(), held_as=jnp.bfloat16):
    level = levels(key, extent, cuts, -0.22, 0.18) if cuts else 1.0
    entries = jax.random.normal(key, extent, jnp.float32) * deviation * level
    return jnp.minimum(jnp.maximum(entries, -most), most).astype(held_as)


def setup_inputs(seed: int = 0) -> dict:
    splits = jax.random.split(jax.random.key(seed), 5)
    return {
        "inputs": gaussian(splits[0], (TOKENS, D), 1.0, 6.0, ((0, 16), (1, 16))),
        "first_weight": gaussian(splits[1], (D, FF), D ** -0.5, 0.0546875, ((0, 16), (1, 16))),
        "second_weight": gaussian(splits[2], (FF, D), FF ** -0.5, 0.02734375, ((0, 16), (1, 16))),
        "cotangent": gaussian(splits[3], (TOKENS, D), 1.0, 6.0, ((0, 16), (1, 16))),
    }


def gelu_both(pre_act, grad_act):
    factor = 0.7978845608028654
    tangent = jnp.tanh(factor * (pre_act + 0.044715 * pre_act * pre_act * pre_act))
    activated = (0.5 * pre_act * (1.0 + tangent)).astype(jnp.bfloat16)
    derivative = 0.5 * (1.0 + tangent) + 0.5 * pre_act * (1.0 - tangent * tangent) * factor * (1.0 + 3.0 * 0.044715 * pre_act * pre_act)
    grad_pre = (grad_act * derivative).astype(jnp.bfloat16)
    return activated, grad_pre


def reference(inputs, first_weight, second_weight, cotangent):
    pre_act = jnp.dot(inputs, first_weight, preferred_element_type=jnp.float32)
    grad_act = lax.dot_general(cotangent, second_weight, (((1,), (1,)), ((), ())), preferred_element_type=jnp.float32)
    activated, grad_pre = gelu_both(pre_act, grad_act)
    output = jnp.dot(activated, second_weight, preferred_element_type=jnp.float32).astype(jnp.bfloat16)
    grad_inputs = lax.dot_general(grad_pre, first_weight, (((1,), (1,)), ((), ())), preferred_element_type=jnp.float32).astype(jnp.bfloat16)
    return output, grad_inputs
```

```python
import jax
import jax.numpy as jnp
from jax import lax
from jax.experimental import pallas as pl
from jax.experimental.pallas import tpu as pltpu
from jax.sharding import PartitionSpec as P

NZ, NY, NX = 8, 4, 4
GROUPS = ((0,), (2,), (1, 3))
BACK = ((2,), (1, 3), (0,))
BF16, F32 = jnp.bfloat16, jnp.float32
VMEM_LIMIT = 40 * 2**20


def hop(value):
    moves = [(2 * z, 2 * ((z + 1) % NZ)) for z in range(NZ)]
    moves += [(2 * z + 1, 2 * ((z - 1) % NZ) + 1) for z in range(NZ)]
    return lax.ppermute(value, "row", moves)


def along_x(value, step):
    moves = [(NX * y + x, NX * y + (x + step) % NX) for y in range(NY) for x in range(NX)]
    return lax.ppermute(value, "col", moves)


def along_y(value, step):
    moves = [(NX * y + x, NX * ((y + step) % NY) + x) for y in range(NY) for x in range(NX)]
    return lax.ppermute(value, "col", moves)


def to_sibling(value):
    return lax.ppermute(value, "row", [(i, i ^ 1) for i in range(2 * NZ)])


def gelu_both(pre_act, grad_act):
    factor = 0.7978845608028654
    tangent = jnp.tanh(factor * (pre_act + 0.044715 * pre_act * pre_act * pre_act))
    activated = (0.5 * pre_act * (1.0 + tangent)).astype(BF16)
    derivative = 0.5 * (1.0 + tangent) + 0.5 * pre_act * (1.0 - tangent * tangent) * factor * (
        1.0 + 3.0 * 0.044715 * pre_act * pre_act
    )
    return activated, (grad_act * derivative).astype(BF16)


def dot(left, right):
    return jnp.dot(left, right, preferred_element_type=F32)


def dot_t(left, right):
    return lax.dot_general(left, right, (((1,), (1,)), ((), ())), preferred_element_type=F32)


def pick(step, table):
    value = jnp.int32(table[0])
    for place, entry in enumerate(table):
        value = jnp.where(step == place, entry, value)
    return value


FIRST = (4, 3, -3, 2, -2, 1, -1, 0)
FIRST_SLOT = (3, 3, 3, 2, 2, 1, 1, 0)
SECOND = (0, -1, 1, -2, 2, -3, 3, 4)


def weight_specs(table, depth, piece):
    def at(step, where_ref):
        return lax.rem(where_ref[0] + where_ref[1] * pick(step, table) + 2 * NZ, NZ)

    return [
        pl.BlockSpec((depth, piece), lambda j, where_ref: (0, at(j, where_ref))),
        pl.BlockSpec((piece, depth), lambda j, where_ref: (at(j, where_ref), 0)),
    ]


def hidden_kernel(where_ref, x_ref, w1_ref, w2_ref, keep_ref, send_ref, keep4_ref, send4_ref):
    step = pl.program_id(0)
    half = keep4_ref.shape[1]
    first = where_ref[1] == 1
    both = (dot(x_ref[0], w1_ref[...]), dot_t(x_ref[1], w2_ref[...]))

    @pl.when(step == 0)
    def _():
        for i, value in enumerate(both):
            keep4_ref[i] = jnp.where(first, value[:half], value[half:])
            send4_ref[i] = jnp.where(first, value[half:], value[:half])

    @pl.when((step % 2 == 1) | (step == 7))
    def _():
        for i, value in enumerate(both):
            keep_ref[0, i] = value

    @pl.when((step > 0) & (step % 2 == 0) | (step == 7))
    def _():
        for i, value in enumerate(both):
            send_ref[0, i] = value


def hidden_terms(where, tokens, w1, w2):
    rows, depth = tokens.shape[1:]
    width = w1.shape[1]
    piece = width // NZ
    out = jax.ShapeDtypeStruct((4, 2, rows, piece), F32)
    out4 = jax.ShapeDtypeStruct((2, rows // 2, piece), F32)
    out_spec = pl.BlockSpec((1, 2, rows, piece), lambda j, where_ref: (pick(j, FIRST_SLOT), 0, 0, 0))
    out4_spec = pl.BlockSpec((2, rows // 2, piece), lambda j, where_ref: (0, 0, 0))
    return pl.pallas_call(
        hidden_kernel,
        grid_spec=pltpu.PrefetchScalarGridSpec(
            num_scalar_prefetch=1,
            grid=(NZ,),
            in_specs=[pl.BlockSpec((2, rows, depth), lambda j, where_ref: (0, 0, 0))]
            + weight_specs(FIRST, depth, piece),
            out_specs=[out_spec, out_spec, out4_spec, out4_spec],
        ),
        out_shape=[out, out, out4, out4],
        cost_estimate=pl.CostEstimate(
            flops=4 * rows * depth * width, bytes_accessed=4 * depth * width + 8 * rows * width, transcendentals=0
        ),
        compiler_params=pltpu.CompilerParams(vmem_limit_bytes=VMEM_LIMIT),
        name="hidden_terms",
    )(where, tokens, w1, w2)


def output_kernel(where_ref, own_ref, near_ref, near_sib_ref, far_ref, far_sib_ref, w1_ref, w2_ref, out_ref):
    step = pl.program_id(0)
    rows = own_ref.shape[1]
    first = where_ref[1] == 1

    def add(forward, backward):
        out_ref[0] += dot(forward, w2_ref[...])
        out_ref[1] += dot_t(backward, w1_ref[...])

    @pl.when(step == 0)
    def _():
        out_ref[0] = dot(own_ref[0], w2_ref[...])
        out_ref[1] = dot_t(own_ref[1], w1_ref[...])

    for at, ref in ((1, near_ref), (2, near_sib_ref)):
        for f in range(2):
            pl.when(step == at + 2 * f)(lambda ref=ref, f=f: add(ref[f, 0], ref[f, 1]))
    for at, ref in ((5, far_ref), (6, far_sib_ref)):
        pl.when(step == at)(lambda ref=ref: add(ref[0, :rows], ref[1, :rows]))

    @pl.when(step == 7)
    def _():
        def halves(i):
            mine, other = far_ref[i, rows:], far_sib_ref[i, rows:]
            return jnp.concatenate([jnp.where(first, mine, other), jnp.where(first, other, mine)], axis=0)

        add(halves(0), halves(1))


def output_terms(where, own, near, near_sib, far, far_sib, w1, w2):
    rows, piece = own.shape[1:]
    depth, width = w1.shape
    whole = lambda value: pl.BlockSpec(value.shape, lambda j, where_ref: (0,) * value.ndim)
    out = jax.ShapeDtypeStruct((2, rows, depth), F32)
    operands = (own, near, near_sib, far, far_sib)
    return pl.pallas_call(
        output_kernel,
        grid_spec=pltpu.PrefetchScalarGridSpec(
            num_scalar_prefetch=1,
            grid=(NZ,),
            in_specs=[whole(value) for value in operands] + weight_specs(SECOND, depth, piece),
            out_specs=whole(out),
        ),
        out_shape=out,
        cost_estimate=pl.CostEstimate(
            flops=4 * rows * depth * width, bytes_accessed=4 * depth * width + 4 * rows * width, transcendentals=0
        ),
        compiler_params=pltpu.CompilerParams(vmem_limit_bytes=VMEM_LIMIT),
        name="output_terms",
    )(where, *operands, w1, w2)


def summed_over_z(first, terms):
    keep, send, keep4, send4 = terms
    sib, sib4 = to_sibling(send), to_sibling(send4)
    arrived = hop((keep4 + sib4).astype(BF16)).astype(F32)
    blank = jnp.zeros_like(arrived)
    arrived = jnp.where(
        first, jnp.concatenate([arrived, blank], axis=1), jnp.concatenate([blank, arrived], axis=1)
    )
    for far in (3, 2, 1):
        arrived = hop((arrived + (keep[far] + sib[far])).astype(BF16)).astype(F32)
    other = to_sibling(arrived.astype(BF16)).astype(F32)
    return (keep[0] + sib[0]) + (arrived + other)


def gathered_over_z(first, own):
    half = own.shape[1] // 2
    one = hop(own)
    two = hop(one)
    three = hop(two)
    four = hop(jnp.where(first, three[:, :half], three[:, half:]))
    near, far = jnp.stack([one, two]), jnp.concatenate([three, four], axis=1)
    return own, near, to_sibling(near), far, to_sibling(far)


def per_device(inputs, w1, w2, cotangent):
    row = lax.axis_index("row")
    first = row % 2 == 0
    where = jnp.stack([row // 2, 1 - 2 * (row % 2)]).astype(jnp.int32)
    own = jnp.stack([inputs, cotangent])
    block, depth = inputs.shape
    rows = NX * block

    here = jnp.concatenate([own] + [along_x(own, -r) for r in (1, 2, 3)], axis=1)
    by_y = {0: here}
    for k in (2, 1, 3):
        by_y[k] = along_y(here, -k)

    acts = {}
    for group in GROUPS:
        tokens = jnp.concatenate([by_y[k] for k in group], axis=1)
        both = summed_over_z(first, hidden_terms(where, tokens, w1, w2))
        acts[group] = jnp.stack(gelu_both(both[0], both[1]))

    outs = {}
    for group in BACK:
        out = output_terms(where, *gathered_over_z(first, acts[group]), w1, w2)
        for at, k in enumerate(group):
            outs[k] = out[:, at * rows : (at + 1) * rows]

    total = outs[0]
    for k in (2, 1, 3):
        total = total + along_y(outs[k], k)
    final = total[:, :block]
    for r in (1, 2, 3):
        final = final + along_x(total[:, r * block : (r + 1) * block], r)
    return final[0].astype(BF16), final[1].astype(BF16)


def solution(mesh):
    return jax.shard_map(
        per_device,
        mesh=mesh,
        in_specs=(P("col", "row"), P("row", "col"), P("col", "row"), P("col", "row")),
        out_specs=(P("col", "row"), P("col", "row")),
        check_vma=False,
    )
```

```python
import functools

import jax
import jax.numpy as jnp
from jax import lax
from jax.experimental import pallas as pl
from jax.experimental.pallas import tpu as pltpu
from jax.sharding import PartitionSpec as P

NZ, NY, NX = 8, 4, 4
GROUPS = {"A": (0,), "B": (1, 3), "C": (2,)}
ORDER = "aAbAAcBABCBCBCACBACBCBCBCAA"
WINDOW = 3
BF16, F32 = jnp.bfloat16, jnp.float32
VMEM_LIMIT = 28 * 2**20
LIGHT = pl.CostEstimate(flops=1, bytes_accessed=1, transcendentals=0)


def hop(value):
    moves = [(2 * z, 2 * ((z + 1) % NZ)) for z in range(NZ)]
    moves += [(2 * z + 1, 2 * ((z - 1) % NZ) + 1) for z in range(NZ)]
    return lax.ppermute(value, "row", moves)


def along_x(value, step):
    moves = [(NX * y + x, NX * y + (x + step) % NX) for y in range(NY) for x in range(NX)]
    return lax.ppermute(value, "col", moves)


def along_y(value, step):
    moves = [(NX * y + x, NX * ((y + step) % NY) + x) for y in range(NY) for x in range(NX)]
    return lax.ppermute(value, "col", moves)


def to_sibling(value):
    return lax.ppermute(value, "row", [(i, i ^ 1) for i in range(2 * NZ)])


def gelu_both(pre_act, grad_act):
    factor = 0.7978845608028654
    tangent = jnp.tanh(factor * (pre_act + 0.044715 * pre_act * pre_act * pre_act))
    activated = (0.5 * pre_act * (1.0 + tangent)).astype(BF16)
    derivative = 0.5 * (1.0 + tangent) + 0.5 * pre_act * (1.0 - tangent * tangent) * factor * (
        1.0 + 3.0 * 0.044715 * pre_act * pre_act
    )
    return activated, (grad_act * derivative).astype(BF16)


def dot(left, right):
    return jnp.dot(left, right, preferred_element_type=F32)


def dot_t(left, right):
    return lax.dot_general(left, right, (((1,), (1,)), ((), ())), preferred_element_type=F32)


FIRST = (4, 0, -3, -2, -1, 3, 2, 1)
NEAR = (0, -1, 1, -2, 2)
FAR = (-3, 3, 4)


def arrange_kernel(where_ref, w1_ref, w2_ref, out1_ref, out2_ref, sems):
    piece = out1_ref.shape[2]
    copies = []
    for j, distance in enumerate(FIRST):
        at = lax.rem(where_ref[0] + where_ref[1] * distance + 2 * NZ, NZ)
        place = pl.ds(pl.multiple_of(at * piece, piece), piece)
        copies.append(pltpu.make_async_copy(w1_ref.at[:, place], out1_ref.at[j], sems.at[0, j]))
        copies.append(pltpu.make_async_copy(w2_ref.at[place, :], out2_ref.at[j], sems.at[1, j]))
    for copy in copies:
        copy.start()
    for copy in copies:
        copy.wait()


def arranged(where, w1, w2):
    depth, width = w1.shape
    piece = width // NZ
    return pl.pallas_call(
        arrange_kernel,
        in_specs=[pl.BlockSpec(memory_space=pltpu.SMEM)] + [pl.BlockSpec(memory_space=pl.ANY)] * 2,
        out_specs=[pl.BlockSpec(memory_space=pl.ANY)] * 2,
        out_shape=[
            jax.ShapeDtypeStruct((NZ, depth, piece), BF16),
            jax.ShapeDtypeStruct((NZ, piece, depth), BF16),
        ],
        scratch_shapes=[pltpu.SemaphoreType.DMA((2, NZ))],
        cost_estimate=LIGHT,
        name="arranged",
    )(where, w1, w2)


def start_pieces(step, table, w1_ref, w2_ref, w1_buf, w2_buf, sems):
    @pl.when(step == 0)
    def _():
        for j, distance in enumerate(table):
            at = FIRST.index(distance)
            pltpu.make_async_copy(w1_ref.at[at], w1_buf.at[j], sems.at[0, j]).start()
            pltpu.make_async_copy(w2_ref.at[at], w2_buf.at[j], sems.at[1, j]).start()


def wait_piece(step, w1_ref, w2_ref, w1_buf, w2_buf, sems):
    pltpu.make_async_copy(w1_ref.at[0], w1_buf.at[step], sems.at[0, step]).wait()
    pltpu.make_async_copy(w2_ref.at[0], w2_buf.at[step], sems.at[1, step]).wait()


def weight_buffers(count, depth, piece):
    return [
        pltpu.VMEM((count, depth, piece), BF16),
        pltpu.VMEM((count, piece, depth), BF16),
        pltpu.SemaphoreType.DMA((2, count)),
    ]


def hidden_kernel(where_ref, x_ref, w1_ref, w2_ref, four_ref, send_ref, keep_ref, w1_buf, w2_buf, sems):
    step = pl.program_id(0)
    weights = (w1_ref, w2_ref, w1_buf, w2_buf, sems)
    start_pieces(step, FIRST, *weights)
    wait_piece(step, *weights)

    @pl.when(step == 0)
    def _():
        four_ref[0] = dot(x_ref[0], w1_buf[0])
        four_ref[1] = dot_t(x_ref[1], w2_buf[0])

    @pl.when((step > 0) & (step < 5))
    def _():
        send_ref[0, 0] = dot(x_ref[0], w1_buf[step])
        send_ref[0, 1] = dot_t(x_ref[1], w2_buf[step])

    @pl.when(step >= 5)
    def _():
        keep_ref[0, 0] = dot(x_ref[0], w1_buf[step])
        keep_ref[0, 1] = dot_t(x_ref[1], w2_buf[step])


def hidden_terms(where, tokens, w1, w2):
    rows, depth = tokens.shape[1:]
    piece = w1.shape[2]
    width = NZ * piece
    out = lambda count: jax.ShapeDtypeStruct((count, 2, rows, piece), F32)
    block = lambda at: pl.BlockSpec((1, 2, rows, piece), lambda j, where_ref: (at(j), 0, 0, 0))
    return pl.pallas_call(
        hidden_kernel,
        grid_spec=pltpu.PrefetchScalarGridSpec(
            num_scalar_prefetch=1,
            grid=(NZ,),
            in_specs=[
                pl.BlockSpec((2, rows, depth), lambda j, where_ref: (0, 0, 0)),
                pl.BlockSpec(memory_space=pl.ANY),
                pl.BlockSpec(memory_space=pl.ANY),
            ],
            out_specs=[
                pl.BlockSpec((2, rows, piece), lambda j, where_ref: (0, 0, 0)),
                block(lambda j: jnp.clip(j - 1, 0, 3)),
                block(lambda j: jnp.maximum(j - 5, 0)),
            ],
            scratch_shapes=weight_buffers(NZ, depth, piece),
        ),
        out_shape=[jax.ShapeDtypeStruct((2, rows, piece), F32), out(4), out(3)],
        cost_estimate=LIGHT,
        compiler_params=pltpu.CompilerParams(vmem_limit_bytes=VMEM_LIMIT),
        name="hidden_terms",
    )(where, tokens, w1, w2)


def add_product(out_ref, forward, backward, w1, w2):
    out_ref[0] += dot(forward, w2)
    out_ref[1] += dot_t(backward, w1)


def near_kernel(where_ref, own_ref, near_ref, sib_ref, w1_ref, w2_ref, out_ref, w1_buf, w2_buf, sems):
    step = pl.program_id(0)
    weights = (w1_ref, w2_ref, w1_buf, w2_buf, sems)
    start_pieces(step, NEAR, *weights)
    wait_piece(step, *weights)

    @pl.when(step == 0)
    def _():
        out_ref[0] = dot(own_ref[0], w2_buf[0])
        out_ref[1] = dot_t(own_ref[1], w1_buf[0])

    for at, ref in ((1, near_ref), (2, sib_ref)):
        @pl.when((step > 0) & (step % 2 == at % 2))
        def _(ref=ref, at=at):
            f = (step - at) // 2
            add_product(out_ref, ref[f, 0], ref[f, 1], w1_buf[step], w2_buf[step])


def far_kernel(
    where_ref, acc_ref, three_ref, three_sib_ref, four_ref, four_sib_ref, w1_ref, w2_ref, out_ref, w1_buf, w2_buf, sems
):
    step = pl.program_id(0)
    first = where_ref[1] == 1
    weights = (w1_ref, w2_ref, w1_buf, w2_buf, sems)
    start_pieces(step, FAR, *weights)
    wait_piece(step, *weights)

    @pl.when(step == 0)
    def _():
        out_ref[...] = acc_ref[...]
        add_product(out_ref, three_ref[0], three_ref[1], w1_buf[0], w2_buf[0])

    @pl.when(step == 1)
    def _():
        add_product(out_ref, three_sib_ref[0], three_sib_ref[1], w1_buf[1], w2_buf[1])

    @pl.when(step == 2)
    def _():
        def halves(i):
            mine, other = four_ref[i], four_sib_ref[i]
            return jnp.concatenate([jnp.where(first, mine, other), jnp.where(first, other, mine)], axis=0)

        add_product(out_ref, halves(0), halves(1), w1_buf[2], w2_buf[2])


def output_terms(kernel, name, count, where, operands, rows, w1, w2):
    depth, piece = w1.shape[1:]
    whole = lambda value: pl.BlockSpec(value.shape, lambda j, where_ref: (0,) * value.ndim)
    out = jax.ShapeDtypeStruct((2, rows, depth), F32)
    return pl.pallas_call(
        kernel,
        grid_spec=pltpu.PrefetchScalarGridSpec(
            num_scalar_prefetch=1,
            grid=(count,),
            in_specs=[whole(value) for value in operands] + [pl.BlockSpec(memory_space=pl.ANY)] * 2,
            out_specs=whole(out),
            scratch_shapes=weight_buffers(count, depth, piece),
        ),
        out_shape=out,
        cost_estimate=LIGHT,
        compiler_params=pltpu.CompilerParams(vmem_limit_bytes=VMEM_LIMIT),
        name=name,
    )(where, *operands, w1, w2)


def after(value, earlier):
    return lax.optimization_barrier((value, earlier))[0]


def group_flow(first, where, parts, w1, w2, marks, earlier):
    tokens = jnp.concatenate(parts, axis=1)
    if earlier is not None:
        tokens = after(tokens, earlier)
    rows = tokens.shape[1]
    half = rows // 2
    four, send, keep = hidden_terms(where, tokens, w1, w2)
    top, bottom = four[:, :half], four[:, half:]
    four_sib = to_sibling(jnp.where(first, bottom, top))
    sib = to_sibling(send)
    marks.append(sib)
    arrived = (yield (jnp.where(first, top, bottom) + four_sib).astype(BF16)).astype(F32)
    blank = jnp.zeros_like(arrived)
    arrived = jnp.where(
        first, jnp.concatenate([arrived, blank], axis=1), jnp.concatenate([blank, arrived], axis=1)
    )
    for i in range(3):
        arrived = (yield (arrived + (keep[i] + sib[i + 1])).astype(BF16)).astype(F32)
    other = to_sibling(arrived.astype(BF16)).astype(F32)
    both = (send[0] + sib[0]) + (arrived + other)
    own = jnp.stack(gelu_both(both[0], both[1]))

    one = yield own
    two = yield one
    near = jnp.stack([one, two])
    operands = (own, near, to_sibling(near))
    out = output_terms(near_kernel, "near_terms", len(NEAR), where, operands, rows, w1, w2)
    three = yield two
    three_sib = to_sibling(three)
    last = yield jnp.where(first, three[:, :half], three[:, half:])
    operands = (out, three, three_sib, last, to_sibling(last))
    return output_terms(far_kernel, "far_terms", len(FAR), where, operands, rows, w1, w2)


def drive(flows, order, window):
    outs, landed, marks, started, waiting = {}, [], [], {}, {}
    for name in order:
        if name.islower():
            name = name.upper()
            started[name] = flows[name](marks, (landed[-1], marks[0]) if landed else None)
            waiting[name] = next(started[name])
            continue
        value = waiting[name]
        if len(landed) >= window:
            value = after(value, landed[-window])
        landed.append(hop(value))
        try:
            waiting[name] = started[name].send(landed[-1])
        except StopIteration as stop:
            outs[name] = stop.value
    return outs


def per_device(inputs, w1, w2, cotangent):
    row = lax.axis_index("row")
    first = row % 2 == 0
    where = jnp.stack([row // 2, 1 - 2 * (row % 2)]).astype(jnp.int32)
    w1, w2 = arranged(where, w1, w2)
    own = jnp.stack([inputs, cotangent])
    block, depth = inputs.shape
    rows = NX * block

    here = jnp.concatenate([own] + [along_x(own, -r) for r in (1, 2, 3)], axis=1)
    by_y = {0: here}
    for k in (1, 3, 2):
        by_y[k] = along_y(here, -k)

    flows = {}
    for name, group in GROUPS.items():
        parts = [by_y[k] for k in group]
        flows[name] = functools.partial(group_flow, first, where, parts, w1, w2)
    finished = drive(flows, ORDER, WINDOW)

    outs = {}
    for name, group in GROUPS.items():
        for at, k in enumerate(group):
            outs[k] = finished[name][:, at * rows : (at + 1) * rows]
    total = outs[0]
    for k in (2, 1, 3):
        total = total + along_y(outs[k].astype(BF16), k).astype(F32)
    final = total[:, :block]
    for r in (1, 2, 3):
        final = final + along_x(total[:, r * block : (r + 1) * block], r)
    return final[0].astype(BF16), final[1].astype(BF16)


def solution(mesh):
    return jax.shard_map(
        per_device,
        mesh=mesh,
        in_specs=(P("col", "row"), P("row", "col"), P("col", "row"), P("col", "row")),
        out_specs=(P("col", "row"), P("col", "row")),
        check_vma=False,
    )
```

```python
import functools

import jax
import jax.numpy as jnp
from jax import lax
from jax.experimental import pallas as pl
from jax.experimental.pallas import tpu as pltpu
from jax.sharding import PartitionSpec as P

NZ, NY, NX = 8, 4, 4
GROUPS = {"P": (0, 1), "Q": (2, 3)}
ORDER = "pPqPQPQPQPQPQPQPQQ"
WINDOW = 2
BF16, F32 = jnp.bfloat16, jnp.float32
VMEM_LIMIT = 50 * 2**20
LIGHT = pl.CostEstimate(flops=1, bytes_accessed=1, transcendentals=0)


def hop(value):
    moves = [(2 * z, 2 * ((z + 1) % NZ)) for z in range(NZ)]
    moves += [(2 * z + 1, 2 * ((z - 1) % NZ) + 1) for z in range(NZ)]
    return lax.ppermute(value, "row", moves)


def along_x(value, step):
    moves = [(NX * y + x, NX * y + (x + step) % NX) for y in range(NY) for x in range(NX)]
    return lax.ppermute(value, "col", moves)


def along_y(value, step):
    moves = [(NX * y + x, NX * ((y + step) % NY) + x) for y in range(NY) for x in range(NX)]
    return lax.ppermute(value, "col", moves)


def to_sibling(value):
    return lax.ppermute(value, "row", [(i, i ^ 1) for i in range(2 * NZ)])


def gelu_both(pre_act, grad_act):
    factor = 0.7978845608028654
    tangent = jnp.tanh(factor * (pre_act + 0.044715 * pre_act * pre_act * pre_act))
    activated = (0.5 * pre_act * (1.0 + tangent)).astype(BF16)
    derivative = 0.5 * (1.0 + tangent) + 0.5 * pre_act * (1.0 - tangent * tangent) * factor * (
        1.0 + 3.0 * 0.044715 * pre_act * pre_act
    )
    return activated, (grad_act * derivative).astype(BF16)


def dot(left, right):
    return jnp.dot(left, right, preferred_element_type=F32)


def dot_t(left, right):
    return lax.dot_general(left, right, (((1,), (1,)), ((), ())), preferred_element_type=F32)


FIRST = (4, 0, -3, -2, -1, 3, 2, 1)
NEAR = (0, -1, 1, -2, 2)
FAR = (-3, 3, 4)


def start_pieces(step, table, where_ref, w1_ref, w2_ref, w1_buf, w2_buf, sems):
    piece = w1_buf.shape[2]

    @pl.when(step == 0)
    def _():
        for j, distance in enumerate(table):
            at = lax.rem(where_ref[0] + where_ref[1] * distance + 2 * NZ, NZ)
            place = pl.ds(pl.multiple_of(at * piece, piece), piece)
            pltpu.make_async_copy(w1_ref.at[:, place], w1_buf.at[j], sems.at[0, j]).start()
            pltpu.make_async_copy(w2_ref.at[place, :], w2_buf.at[j], sems.at[1, j]).start()


def wait_piece(step, w1_ref, w2_ref, w1_buf, w2_buf, sems):
    piece = w1_buf.shape[2]
    pltpu.make_async_copy(w1_ref.at[:, pl.ds(0, piece)], w1_buf.at[step], sems.at[0, step]).wait()
    pltpu.make_async_copy(w2_ref.at[pl.ds(0, piece), :], w2_buf.at[step], sems.at[1, step]).wait()


def weight_buffers(count, depth, piece):
    return [
        pltpu.VMEM((count, depth, piece), BF16),
        pltpu.VMEM((count, piece, depth), BF16),
        pltpu.SemaphoreType.DMA((2, count)),
    ]


def hidden_kernel(where_ref, x_ref, w1_ref, w2_ref, four_ref, send_ref, keep_ref, w1_buf, w2_buf, sems):
    step = pl.program_id(0)
    weights = (w1_ref, w2_ref, w1_buf, w2_buf, sems)
    start_pieces(step, FIRST, where_ref, *weights)
    wait_piece(step, *weights)

    @pl.when(step == 0)
    def _():
        four_ref[0] = dot(x_ref[0], w1_buf[0])
        four_ref[1] = dot_t(x_ref[1], w2_buf[0])

    @pl.when((step > 0) & (step < 5))
    def _():
        send_ref[0, 0] = dot(x_ref[0], w1_buf[step])
        send_ref[0, 1] = dot_t(x_ref[1], w2_buf[step])

    @pl.when(step >= 5)
    def _():
        keep_ref[0, 0] = dot(x_ref[0], w1_buf[step])
        keep_ref[0, 1] = dot_t(x_ref[1], w2_buf[step])


def hidden_terms(where, tokens, w1, w2):
    rows, depth = tokens.shape[1:]
    piece = w1.shape[1] // NZ
    out = lambda count: jax.ShapeDtypeStruct((count, 2, rows, piece), F32)
    block = lambda at: pl.BlockSpec((1, 2, rows, piece), lambda j, where_ref: (at(j), 0, 0, 0))
    return pl.pallas_call(
        hidden_kernel,
        grid_spec=pltpu.PrefetchScalarGridSpec(
            num_scalar_prefetch=1,
            grid=(NZ,),
            in_specs=[
                pl.BlockSpec((2, rows, depth), lambda j, where_ref: (0, 0, 0)),
                pl.BlockSpec(memory_space=pl.ANY),
                pl.BlockSpec(memory_space=pl.ANY),
            ],
            out_specs=[
                pl.BlockSpec((2, rows, piece), lambda j, where_ref: (0, 0, 0)),
                block(lambda j: jnp.clip(j - 1, 0, 3)),
                block(lambda j: jnp.maximum(j - 5, 0)),
            ],
            scratch_shapes=weight_buffers(NZ, depth, piece),
        ),
        out_shape=[jax.ShapeDtypeStruct((2, rows, piece), F32), out(4), out(3)],
        cost_estimate=LIGHT,
        compiler_params=pltpu.CompilerParams(vmem_limit_bytes=VMEM_LIMIT),
        name="hidden_terms",
    )(where, tokens, w1, w2)


def add_product(out_ref, forward, backward, w1, w2):
    out_ref[0] += dot(forward, w2)
    out_ref[1] += dot_t(backward, w1)


def near_kernel(where_ref, own_ref, near_ref, sib_ref, w1_ref, w2_ref, out_ref, w1_buf, w2_buf, sems):
    step = pl.program_id(0)
    weights = (w1_ref, w2_ref, w1_buf, w2_buf, sems)
    start_pieces(step, NEAR, where_ref, *weights)
    wait_piece(step, *weights)

    @pl.when(step == 0)
    def _():
        out_ref[0] = dot(own_ref[0], w2_buf[0])
        out_ref[1] = dot_t(own_ref[1], w1_buf[0])

    for at, ref in ((1, near_ref), (2, sib_ref)):
        @pl.when((step > 0) & (step % 2 == at % 2))
        def _(ref=ref, at=at):
            f = (step - at) // 2
            add_product(out_ref, ref[f, 0], ref[f, 1], w1_buf[step], w2_buf[step])


def far_kernel(
    where_ref, acc_ref, three_ref, three_sib_ref, four_ref, four_sib_ref, w1_ref, w2_ref, out_ref, w1_buf, w2_buf, sems
):
    step = pl.program_id(0)
    first = where_ref[1] == 1
    weights = (w1_ref, w2_ref, w1_buf, w2_buf, sems)
    start_pieces(step, FAR, where_ref, *weights)
    wait_piece(step, *weights)

    @pl.when(step == 0)
    def _():
        out_ref[...] = acc_ref[...]
        add_product(out_ref, three_ref[0], three_ref[1], w1_buf[0], w2_buf[0])

    @pl.when(step == 1)
    def _():
        add_product(out_ref, three_sib_ref[0], three_sib_ref[1], w1_buf[1], w2_buf[1])

    @pl.when(step == 2)
    def _():
        def halves(i):
            mine, other = four_ref[i], four_sib_ref[i]
            return jnp.concatenate([jnp.where(first, mine, other), jnp.where(first, other, mine)], axis=0)

        add_product(out_ref, halves(0), halves(1), w1_buf[2], w2_buf[2])


def output_terms(kernel, name, count, where, operands, rows, w1, w2):
    depth, piece = w1.shape[0], w1.shape[1] // NZ
    whole = lambda value: pl.BlockSpec(value.shape, lambda j, where_ref: (0,) * value.ndim)
    out = jax.ShapeDtypeStruct((2, rows, depth), F32)
    return pl.pallas_call(
        kernel,
        grid_spec=pltpu.PrefetchScalarGridSpec(
            num_scalar_prefetch=1,
            grid=(count,),
            in_specs=[whole(value) for value in operands] + [pl.BlockSpec(memory_space=pl.ANY)] * 2,
            out_specs=whole(out),
            scratch_shapes=weight_buffers(count, depth, piece),
        ),
        out_shape=out,
        cost_estimate=LIGHT,
        compiler_params=pltpu.CompilerParams(vmem_limit_bytes=VMEM_LIMIT),
        name=name,
    )(where, *operands, w1, w2)


def after(value, earlier):
    return lax.optimization_barrier((value, earlier))[0]


def group_flow(first, where, parts, w1, w2, marks, earlier):
    tokens = jnp.concatenate(parts, axis=1)
    if earlier is not None:
        tokens = after(tokens, earlier)
    rows = tokens.shape[1]
    half = rows // 2
    four, send, keep = hidden_terms(where, tokens, w1, w2)
    top, bottom = four[:, :half], four[:, half:]
    four_sib = to_sibling(jnp.where(first, bottom, top))
    sib = to_sibling(after(send, four_sib))
    marks.append(four_sib)
    arrived = (yield (jnp.where(first, top, bottom) + four_sib).astype(BF16)).astype(F32)
    blank = jnp.zeros_like(arrived)
    arrived = jnp.where(
        first, jnp.concatenate([arrived, blank], axis=1), jnp.concatenate([blank, arrived], axis=1)
    )
    for i in range(3):
        arrived = (yield (arrived + (keep[i] + sib[i + 1])).astype(BF16)).astype(F32)
    other = to_sibling(arrived.astype(BF16)).astype(F32)
    both = (send[0] + sib[0]) + (arrived + other)
    own = jnp.stack(gelu_both(both[0], both[1]))

    one = yield own
    two = yield one
    near = jnp.stack([one, two])
    operands = (own, near, to_sibling(near))
    out = output_terms(near_kernel, "near_terms", len(NEAR), where, operands, rows, w1, w2)
    three = yield two
    three_sib = to_sibling(three)
    last = yield jnp.where(first, three[:, :half], three[:, half:])
    operands = (out, three, three_sib, last, to_sibling(last))
    return output_terms(far_kernel, "far_terms", len(FAR), where, operands, rows, w1, w2)


def drive(flows, order, window):
    outs, landed, marks, started, waiting = {}, [], [], {}, {}
    for name in order:
        if name.islower():
            name = name.upper()
            started[name] = flows[name](marks, marks[0] if marks else None)
            waiting[name] = next(started[name])
            continue
        value = waiting[name]
        if len(landed) >= window:
            value = after(value, landed[-window])
        landed.append(hop(value))
        try:
            waiting[name] = started[name].send(landed[-1])
        except StopIteration as stop:
            outs[name] = stop.value
    return outs


def per_device(inputs, w1, w2, cotangent):
    row = lax.axis_index("row")
    first = row % 2 == 0
    where = jnp.stack([row // 2, 1 - 2 * (row % 2)]).astype(jnp.int32)
    own = jnp.stack([inputs, cotangent])
    block, depth = inputs.shape

    here = jnp.concatenate([own] + [along_x(own, -r) for r in (1, 2, 3)], axis=1)
    by_y = {0: here}
    for k in (1, 2, 3):
        by_y[k] = along_y(here, -k)

    flows = {}
    for name, group in GROUPS.items():
        parts = [by_y[k] for k in group]
        flows[name] = functools.partial(group_flow, first, where, parts, w1, w2)
    finished = drive(flows, ORDER, WINDOW)

    sums = {}
    for name, group in GROUPS.items():
        out = finished[name].reshape(2, len(group), NX, block, depth)
        total = out[:, :, 0]
        for r in (2, 1, 3):
            total = total + along_x(out[:, :, r].astype(BF16), r).astype(F32)
        sums.update({k: total[:, at] for at, k in enumerate(group)})
    final = sums[0]
    for k in (1, 2, 3):
        final = final + along_y(sums[k], k)
    return final[0].astype(BF16), final[1].astype(BF16)


def solution(mesh):
    return jax.shard_map(
        per_device,
        mesh=mesh,
        in_specs=(P("col", "row"), P("row", "col"), P("col", "row"), P("col", "row")),
        out_specs=(P("col", "row"), P("col", "row")),
        check_vma=False,
    )
```

```python
import functools

import jax
import jax.numpy as jnp
from jax import lax
from jax.experimental import pallas as pl
from jax.experimental.pallas import tpu as pltpu
from jax.sharding import PartitionSpec as P

NZ, NY, NX = 8, 4, 4
GROUPS = {"P": (0, 1), "Q": (2, 3)}
ORDER = "pPqPQPQPQPQPQPQPQQ"
WINDOW = 2
BF16, F32 = jnp.bfloat16, jnp.float32
VMEM_LIMIT = 50 * 2**20
LIGHT = pl.CostEstimate(flops=1, bytes_accessed=1, transcendentals=0)


def hop(value):
    moves = [(2 * z, 2 * ((z + 1) % NZ)) for z in range(NZ)]
    moves += [(2 * z + 1, 2 * ((z - 1) % NZ) + 1) for z in range(NZ)]
    return lax.ppermute(value, "row", moves)


def along_x(value, step):
    moves = [(NX * y + x, NX * y + (x + step) % NX) for y in range(NY) for x in range(NX)]
    return lax.ppermute(value, "col", moves)


def along_y(value, step):
    moves = [(NX * y + x, NX * ((y + step) % NY) + x) for y in range(NY) for x in range(NX)]
    return lax.ppermute(value, "col", moves)


def to_sibling(value):
    return lax.ppermute(value, "row", [(i, i ^ 1) for i in range(2 * NZ)])


def gelu_both(pre_act, grad_act):
    factor = 0.7978845608028654
    tangent = jnp.tanh(factor * (pre_act + 0.044715 * pre_act * pre_act * pre_act))
    activated = (0.5 * pre_act * (1.0 + tangent)).astype(BF16)
    derivative = 0.5 * (1.0 + tangent) + 0.5 * pre_act * (1.0 - tangent * tangent) * factor * (
        1.0 + 3.0 * 0.044715 * pre_act * pre_act
    )
    return activated, (grad_act * derivative).astype(BF16)


def dot(left, right):
    return jnp.dot(left, right, preferred_element_type=F32)


def dot_t(left, right):
    return lax.dot_general(left, right, (((1,), (1,)), ((), ())), preferred_element_type=F32)


FIRST = (4, 0, -3, -2, -1, 3, 2, 1)
NEAR = (0, -1, 1, -2, 2)
FAR = (-3, 3, 4)


def pick(step, table):
    value = jnp.int32(table[0])
    for place, entry in enumerate(table):
        value = jnp.where(step == place, entry, value)
    return value


def next_piece(step, table, where_ref, w1_ref, w2_ref, w1_buf, w2_buf, sems):
    piece = w1_buf.shape[2]

    def copies(at, slot):
        place = pl.ds(pl.multiple_of(at * piece, piece), piece)
        return (
            pltpu.make_async_copy(w1_ref.at[:, place], w1_buf.at[slot], sems.at[0, slot]),
            pltpu.make_async_copy(w2_ref.at[place, :], w2_buf.at[slot], sems.at[1, slot]),
        )

    def start(of):
        at = lax.rem(where_ref[0] + where_ref[1] * pick(of, table) + 2 * NZ, NZ)
        for copy in copies(at, lax.rem(of, 3)):
            copy.start()

    @pl.when(step == 0)
    def _():
        start(jnp.int32(0))
        start(jnp.int32(1))

    @pl.when(step + 2 < len(table))
    def _():
        start(step + 2)

    slot = lax.rem(step, 3)
    for copy in copies(0, slot):
        copy.wait()
    return slot


def weight_buffers(depth, piece):
    return [
        pltpu.VMEM((3, depth, piece), BF16),
        pltpu.VMEM((3, piece, depth), BF16),
        pltpu.SemaphoreType.DMA((2, 3)),
    ]


def hidden_kernel(where_ref, x_ref, w1_ref, w2_ref, four_ref, send_ref, keep_ref, w1_buf, w2_buf, sems):
    step = pl.program_id(0)
    weights = (w1_ref, w2_ref, w1_buf, w2_buf, sems)
    slot = next_piece(step, FIRST, where_ref, *weights)

    @pl.when(step == 0)
    def _():
        four_ref[0] = dot(x_ref[0], w1_buf[slot])
        four_ref[1] = dot_t(x_ref[1], w2_buf[slot])

    @pl.when((step > 0) & (step < 5))
    def _():
        send_ref[0, 0] = dot(x_ref[0], w1_buf[slot])
        send_ref[0, 1] = dot_t(x_ref[1], w2_buf[slot])

    @pl.when(step >= 5)
    def _():
        keep_ref[0, 0] = dot(x_ref[0], w1_buf[slot])
        keep_ref[0, 1] = dot_t(x_ref[1], w2_buf[slot])


def hidden_terms(where, tokens, w1, w2):
    rows, depth = tokens.shape[1:]
    piece = w1.shape[1] // NZ
    out = lambda count: jax.ShapeDtypeStruct((count, 2, rows, piece), F32)
    block = lambda at: pl.BlockSpec((1, 2, rows, piece), lambda j, where_ref: (at(j), 0, 0, 0))
    return pl.pallas_call(
        hidden_kernel,
        grid_spec=pltpu.PrefetchScalarGridSpec(
            num_scalar_prefetch=1,
            grid=(NZ,),
            in_specs=[
                pl.BlockSpec((2, rows, depth), lambda j, where_ref: (0, 0, 0)),
                pl.BlockSpec(memory_space=pl.ANY),
                pl.BlockSpec(memory_space=pl.ANY),
            ],
            out_specs=[
                pl.BlockSpec((2, rows, piece), lambda j, where_ref: (0, 0, 0)),
                block(lambda j: jnp.clip(j - 1, 0, 3)),
                block(lambda j: jnp.maximum(j - 5, 0)),
            ],
            scratch_shapes=weight_buffers(depth, piece),
        ),
        out_shape=[jax.ShapeDtypeStruct((2, rows, piece), F32), out(4), out(3)],
        cost_estimate=LIGHT,
        compiler_params=pltpu.CompilerParams(vmem_limit_bytes=VMEM_LIMIT),
        name="hidden_terms",
    )(where, tokens, w1, w2)


def add_product(out_ref, forward, backward, w1, w2):
    out_ref[0] += dot(forward, w2)
    out_ref[1] += dot_t(backward, w1)


def near_kernel(where_ref, own_ref, near_ref, sib_ref, w1_ref, w2_ref, out_ref, w1_buf, w2_buf, sems):
    step = pl.program_id(0)
    weights = (w1_ref, w2_ref, w1_buf, w2_buf, sems)
    slot = next_piece(step, NEAR, where_ref, *weights)

    @pl.when(step == 0)
    def _():
        out_ref[0] = dot(own_ref[0], w2_buf[slot])
        out_ref[1] = dot_t(own_ref[1], w1_buf[slot])

    for at, ref in ((1, near_ref), (2, sib_ref)):
        @pl.when((step > 0) & (step % 2 == at % 2))
        def _(ref=ref, at=at):
            f = (step - at) // 2
            add_product(out_ref, ref[f, 0], ref[f, 1], w1_buf[slot], w2_buf[slot])


def far_kernel(
    where_ref, acc_ref, three_ref, three_sib_ref, four_ref, four_sib_ref, w1_ref, w2_ref, out_ref, w1_buf, w2_buf, sems
):
    step = pl.program_id(0)
    first = where_ref[1] == 1
    weights = (w1_ref, w2_ref, w1_buf, w2_buf, sems)
    slot = next_piece(step, FAR, where_ref, *weights)

    @pl.when(step == 0)
    def _():
        out_ref[...] = acc_ref[...]
        add_product(out_ref, three_ref[0], three_ref[1], w1_buf[slot], w2_buf[slot])

    @pl.when(step == 1)
    def _():
        add_product(out_ref, three_sib_ref[0], three_sib_ref[1], w1_buf[slot], w2_buf[slot])

    @pl.when(step == 2)
    def _():
        def halves(i):
            mine, other = four_ref[i], four_sib_ref[i]
            return jnp.concatenate([jnp.where(first, mine, other), jnp.where(first, other, mine)], axis=0)

        add_product(out_ref, halves(0), halves(1), w1_buf[slot], w2_buf[slot])


def output_terms(kernel, name, count, where, operands, rows, w1, w2):
    depth, piece = w1.shape[0], w1.shape[1] // NZ
    whole = lambda value: pl.BlockSpec(value.shape, lambda j, where_ref: (0,) * value.ndim)
    out = jax.ShapeDtypeStruct((2, rows, depth), F32)
    return pl.pallas_call(
        kernel,
        grid_spec=pltpu.PrefetchScalarGridSpec(
            num_scalar_prefetch=1,
            grid=(count,),
            in_specs=[whole(value) for value in operands] + [pl.BlockSpec(memory_space=pl.ANY)] * 2,
            out_specs=whole(out),
            scratch_shapes=weight_buffers(depth, piece),
        ),
        out_shape=out,
        input_output_aliases={1: 0} if count == len(FAR) else {},
        cost_estimate=LIGHT,
        compiler_params=pltpu.CompilerParams(vmem_limit_bytes=VMEM_LIMIT),
        name=name,
    )(where, *operands, w1, w2)


def after(value, earlier):
    return lax.optimization_barrier((value, earlier))[0]


def group_flow(first, where, parts, w1, w2, earlier):
    tokens = jnp.concatenate(parts, axis=1)
    if earlier is not None:
        tokens = after(tokens, earlier)
    rows = tokens.shape[1]
    half = rows // 2
    four, send, keep = hidden_terms(where, tokens, w1, w2)
    top, bottom = four[:, :half], four[:, half:]
    four_sib = to_sibling(jnp.where(first, bottom, top))
    sib = to_sibling(after(send, four_sib))
    start = (jnp.where(first, top, bottom) + four_sib).astype(BF16)
    arrived = yield (start[0], start[1])

    def placed(value):
        value = value.astype(F32)
        blank = jnp.zeros_like(value)
        above, below = jnp.concatenate([value, blank], axis=0), jnp.concatenate([blank, value], axis=0)
        return jnp.where(first, above, below)

    arrived = [placed(value) for value in arrived]
    for i in range(3):
        arrived = yield [(arrived[t].astype(F32) + (keep[i, t] + sib[i + 1, t])).astype(BF16) for t in range(2)]
    other = to_sibling(jnp.stack(arrived))
    both = [(send[0, t] + sib[0, t]) + (arrived[t].astype(F32) + other[t].astype(F32)) for t in range(2)]
    own = gelu_both(*both)

    one = yield own
    two = yield one
    near = jnp.stack([jnp.stack(one), jnp.stack(two)])
    operands = (jnp.stack(own), near, to_sibling(near))
    out = output_terms(near_kernel, "near_terms", len(NEAR), where, operands, rows, w1, w2)
    three = yield two
    three_sib = to_sibling(jnp.stack(three))
    last = yield [jnp.where(first, value[:half], value[half:]) for value in three]
    last = jnp.stack(last)
    operands = (out, jnp.stack(three), three_sib, last, to_sibling(last))
    return output_terms(far_kernel, "far_terms", len(FAR), where, operands, rows, w1, w2)


def drive(flows, order, window):
    outs, landed, started, waiting = {}, [], {}, {}
    for name in order:
        if name.islower():
            name = name.upper()
            started[name] = flows[name](landed[-1] if landed else None)
            waiting[name] = next(started[name])
            continue
        value = tuple(waiting[name])
        if len(landed) >= window:
            value = after(value, landed[-window])
        landed.append([hop(each) for each in value])
        try:
            waiting[name] = started[name].send(landed[-1])
        except StopIteration as stop:
            outs[name] = stop.value
    return outs


def per_device(inputs, w1, w2, cotangent):
    row = lax.axis_index("row")
    first = row % 2 == 0
    where = jnp.stack([row // 2, 1 - 2 * (row % 2)]).astype(jnp.int32)
    own = jnp.stack([inputs, cotangent])
    block, depth = inputs.shape

    here = jnp.concatenate([own] + [along_x(own, -r) for r in (1, 2, 3)], axis=1)
    by_y = {0: here, 1: along_y(here, -1), 3: along_y(here, 1)}
    by_y[1], by_y[3] = lax.optimization_barrier((by_y[1], by_y[3]))
    by_y[2] = along_y(after(here, by_y[1]), -2)

    flows = {}
    for name, group in GROUPS.items():
        parts = [by_y[k] for k in group]
        flows[name] = functools.partial(group_flow, first, where, parts, w1, w2)
    finished = drive(flows, ORDER, WINDOW)

    sums = {}
    for name, group in GROUPS.items():
        out = finished[name].reshape(2, len(group), NX, block, depth)
        total = out[:, :, 0]
        for r in (2, 1, 3):
            total = total + along_x(out[:, :, r].astype(BF16), r).astype(F32)
        sums.update({k: total[:, at] for at, k in enumerate(group)})
    final = sums[0]
    for k in (1, 2, 3):
        final = final + along_y(sums[k], k)
    return final[0].astype(BF16), final[1].astype(BF16)


def solution(mesh):
    return jax.shard_map(
        per_device,
        mesh=mesh,
        in_specs=(P("col", "row"), P("row", "col"), P("col", "row"), P("col", "row")),
        out_specs=(P("col", "row"), P("col", "row")),
        check_vma=False,
    )
```

```python
import functools

import jax
import jax.numpy as jnp
from jax import lax
from jax.experimental import pallas as pl
from jax.experimental.pallas import tpu as pltpu
from jax.sharding import PartitionSpec as P

NZ, NY, NX = 8, 4, 4
BF16, F32 = jnp.bfloat16, jnp.float32
VMEM_LIMIT = 20 * 2**20
LIGHT = pl.CostEstimate(flops=1, bytes_accessed=1, transcendentals=0)
HEAVY = pl.CostEstimate(flops=4 * 512 * 768 * 5 * 384, bytes_accessed=5 * 2**22, transcendentals=0)


def along_z(value, step):
    moves = [(2 * z + c, 2 * ((z + step) % NZ) + c) for z in range(NZ) for c in range(2)]
    return lax.ppermute(value, "row", moves)


def along_x(value, step):
    moves = [(NX * y + x, NX * y + (x + step) % NX) for y in range(NY) for x in range(NX)]
    return lax.ppermute(value, "col", moves)


def along_y(value, step):
    moves = [(NX * y + x, NX * ((y + step) % NY) + x) for y in range(NY) for x in range(NX)]
    return lax.ppermute(value, "col", moves)


def to_sibling(value):
    return lax.ppermute(value, "row", [(i, i ^ 1) for i in range(2 * NZ)])


def after(value, earlier):
    return lax.optimization_barrier((value, earlier))[0]


def gelu_both(pre_act, grad_act):
    factor = 0.7978845608028654
    tangent = jnp.tanh(factor * (pre_act + 0.044715 * pre_act * pre_act * pre_act))
    activated = (0.5 * pre_act * (1.0 + tangent)).astype(BF16)
    derivative = 0.5 * (1.0 + tangent) + 0.5 * pre_act * (1.0 - tangent * tangent) * factor * (
        1.0 + 3.0 * 0.044715 * pre_act * pre_act
    )
    return activated, (grad_act * derivative).astype(BF16)


def dot(left, right):
    return jnp.dot(left, right, preferred_element_type=F32)


def dot_t(left, right):
    return lax.dot_general(left, right, (((1,), (1,)), ((), ())), preferred_element_type=F32)


FIRST, SECOND = (4, 3, 5), (2, 6, 1, 7, 0)
NEAR, FAR = (0, 7, 1, 6, 2), (5, 3, 4)


def pick(step, table):
    value = jnp.int32(table[0])
    for place, entry in enumerate(table):
        value = jnp.where(step == place, entry, value)
    return value


def next_piece(step, table, where_ref, w1_ref, w2_ref, w1_buf, w2_buf, sems):
    piece = w1_buf.shape[2]

    def copies(at, slot):
        place = pl.ds(pl.multiple_of(at * piece, piece), piece)
        return (
            pltpu.make_async_copy(w1_ref.at[:, place], w1_buf.at[slot], sems.at[0, slot]),
            pltpu.make_async_copy(w2_ref.at[place, :], w2_buf.at[slot], sems.at[1, slot]),
        )

    def start(of):
        at = lax.rem(where_ref[0] + pick(of, table), NZ)
        for copy in copies(at, lax.rem(of, 3)):
            copy.start()

    @pl.when(step == 0)
    def _():
        start(jnp.int32(0))
        start(jnp.int32(1))

    @pl.when(step + 2 < len(table))
    def _():
        start(step + 2)

    slot = lax.rem(step, 3)
    for copy in copies(0, slot):
        copy.wait()
    return slot


def weight_buffers(depth, piece):
    return [
        pltpu.VMEM((3, depth, piece), BF16),
        pltpu.VMEM((3, piece, depth), BF16),
        pltpu.SemaphoreType.DMA((2, 3)),
    ]


def hidden_kernel(table, where_ref, x_ref, w1_ref, w2_ref, mine_ref, other_ref, w1_buf, w2_buf, sems):
    slot = next_piece(pl.program_id(0), table, where_ref, w1_ref, w2_ref, w1_buf, w2_buf, sems)
    half = mine_ref.shape[2]
    forward = dot(x_ref[0], w1_buf[slot])
    mine_ref[0, 0] = forward[:half]
    other_ref[0, 0] = forward[half:]
    backward = dot_t(x_ref[1], w2_buf[slot])
    mine_ref[0, 1] = backward[:half]
    other_ref[0, 1] = backward[half:]


def call(kernel, name, table, where, operands, specs, w1, w2, out_shape, out_specs, **more):
    depth, piece = w1.shape[0], w1.shape[1] // NZ
    return pl.pallas_call(
        functools.partial(kernel, table),
        grid_spec=pltpu.PrefetchScalarGridSpec(
            num_scalar_prefetch=1,
            grid=(len(table),),
            in_specs=specs + [pl.BlockSpec(memory_space=pl.ANY)] * 2,
            out_specs=out_specs,
            scratch_shapes=weight_buffers(depth, piece),
        ),
        out_shape=out_shape,
        cost_estimate=HEAVY if table == SECOND else LIGHT,
        compiler_params=pltpu.CompilerParams(vmem_limit_bytes=VMEM_LIMIT),
        name=name,
        **more,
    )(where, *operands, w1, w2)


def touch_kernel(where_ref, w1_ref, w2_ref, out_ref):
    out_ref[0] = where_ref[0]


def touched(where, w1, w2):
    return pl.pallas_call(
        touch_kernel,
        in_specs=[pl.BlockSpec(memory_space=pltpu.SMEM)] + [pl.BlockSpec(memory_space=pl.ANY)] * 2,
        out_specs=pl.BlockSpec(memory_space=pltpu.SMEM),
        out_shape=jax.ShapeDtypeStruct((1,), jnp.int32),
        cost_estimate=LIGHT,
        name="touched",
    )(where, w1, w2)


def whole(value):
    return pl.BlockSpec(value.shape, lambda j, where_ref: (0,) * len(value.shape))


def hidden_terms(name, table, where, tokens, w1, w2):
    half, piece = tokens.shape[1] // 2, w1.shape[1] // NZ
    out = jax.ShapeDtypeStruct((len(table), 2, half, piece), F32)
    block = pl.BlockSpec((1, 2, half, piece), lambda j, where_ref: (j, 0, 0, 0))
    mine, other = call(
        hidden_kernel, name, table, where, [tokens], [whole(tokens)], w1, w2, [out, out], [block, block]
    )
    return mine, other


def rows_of(mine_ref, other_ref, *at):
    return jnp.concatenate([mine_ref[at], other_ref[at]], axis=0)


def near_kernel(table, where_ref, mine_ref, other_ref, w1_ref, w2_ref, out_ref, w1_buf, w2_buf, sems):
    step = pl.program_id(0)
    slot = next_piece(step, table, where_ref, w1_ref, w2_ref, w1_buf, w2_buf, sems)
    forward = dot(rows_of(mine_ref, other_ref, 0, 0), w2_buf[slot])
    backward = dot_t(rows_of(mine_ref, other_ref, 0, 1), w1_buf[slot])

    @pl.when(step == 0)
    def _():
        out_ref[0] = forward
        out_ref[1] = backward

    @pl.when(step > 0)
    def _():
        out_ref[0] += forward
        out_ref[1] += backward


def far_kernel(
    table, where_ref, acc_ref, mine3_ref, other3_ref, mine4_ref, other4_ref, w1_ref, w2_ref, out_ref, w1_buf, w2_buf, sems
):
    step = pl.program_id(0)
    slot = next_piece(step, table, where_ref, w1_ref, w2_ref, w1_buf, w2_buf, sems)

    @pl.when(step == 0)
    def _():
        out_ref[...] = acc_ref[...]

    @pl.when(step < 2)
    def _():
        out_ref[0] += dot(rows_of(mine3_ref, other3_ref, step, 0), w2_buf[slot])
        out_ref[1] += dot_t(rows_of(mine3_ref, other3_ref, step, 1), w1_buf[slot])

    @pl.when(step == 2)
    def _():
        out_ref[0] += dot(rows_of(mine4_ref, other4_ref, 0), w2_buf[slot])
        out_ref[1] += dot_t(rows_of(mine4_ref, other4_ref, 1), w1_buf[slot])


def summed_over_z(where, tokens, w1, w2):
    mine, other = hidden_terms("first_terms", FIRST, where, tokens, w1, w2)
    sib = to_sibling(other)
    mine2, other2 = hidden_terms("second_terms", SECOND, where, after(tokens, other), w1, w2)
    sib2 = to_sibling(after(other2, sib))

    def total(j):
        if j in FIRST:
            return mine[FIRST.index(j)] + sib[FIRST.index(j)]
        return mine2[SECOND.index(j)] + sib2[SECOND.index(j)]

    quarter = mine.shape[2] // 2
    start = total(4).astype(BF16)
    up, down = along_z(start[:, :quarter], 1).astype(F32), along_z(start[:, quarter:], -1).astype(F32)
    blank = jnp.zeros_like(up)
    up, down = jnp.concatenate([up, blank], axis=1), jnp.concatenate([blank, down], axis=1)
    for far in (3, 2, 1):
        up = along_z((up + total(far)).astype(BF16), 1).astype(F32)
        down = along_z((down + total(NZ - far)).astype(BF16), -1).astype(F32)
    return total(0) + (up + down)


def output_terms(where, own, w1, w2):
    quarter = own.shape[1] // 2
    depth = w1.shape[0]
    ups, downs = [own], [own]
    for _ in range(3):
        ups.append(along_z(ups[-1], 1))
        downs.append(along_z(downs[-1], -1))
    near = jnp.stack([own, ups[1], downs[1], ups[2], downs[2]])
    near_sib = to_sibling(near)
    three = jnp.stack([ups[3], downs[3]])
    three_sib = to_sibling(three)
    four = along_z(ups[3][:, :quarter], 1), along_z(downs[3][:, quarter:], -1)

    out = jax.ShapeDtypeStruct((2, 2 * own.shape[1], depth), F32)
    block = pl.BlockSpec((1, *own.shape), lambda j, where_ref: (j, 0, 0, 0))
    acc = call(near_kernel, "near_terms", NEAR, where, [near, near_sib], [block, block], w1, w2, out, whole(out))
    four = jnp.concatenate(after(four, acc), axis=1)
    four_sib = to_sibling(four)
    operands = [acc, three, three_sib, four, four_sib]
    return call(
        far_kernel, "far_terms", FAR, where, operands, [whole(value) for value in operands], w1, w2, out, whole(out),
        input_output_aliases={1: 0},
    )


def per_device(inputs, w1, w2, cotangent):
    row = lax.axis_index("row")
    first = row % 2 == 0
    where = touched((row // 2).astype(jnp.int32).reshape(1), w1, w2)
    own = jnp.stack([inputs, cotangent])
    block, depth = inputs.shape

    by_x = [own] + [along_x(own, -r) for r in (1, 2, 3)]
    low, high = jnp.stack(by_x[:2], axis=1), jnp.stack(by_x[2:], axis=1)
    here = jnp.stack([jnp.where(first, low, high), jnp.where(first, high, low)], axis=1)
    by_y = [here] + [along_y(here, -k) for k in (1, 2, 3)]
    tokens = jnp.stack(by_y, axis=2).reshape(2, NY * NX * block, depth)

    both = summed_over_z(where, tokens, w1, w2)
    out = output_terms(where, jnp.stack(gelu_both(both[0], both[1])), w1, w2)

    out = out.reshape(2, 2, NY, 2, block, depth)
    low, high = jnp.where(first, out[:, 0], out[:, 1]), jnp.where(first, out[:, 1], out[:, 0])
    by_x = [low[:, :, 0], low[:, :, 1], high[:, :, 0], high[:, :, 1]]
    total = by_x[0]
    for r in (2, 1, 3):
        total = total + along_x(by_x[r].astype(BF16), r).astype(F32)
    final = total[:, 0]
    for k in (2, 1, 3):
        final = final + along_y(total[:, k], k)
    return final[0].astype(BF16), final[1].astype(BF16)


def solution(mesh):
    return jax.shard_map(
        per_device,
        mesh=mesh,
        in_specs=(P("col", "row"), P("row", "col"), P("col", "row"), P("col", "row")),
        out_specs=(P("col", "row"), P("col", "row")),
        check_vma=False,
    )
```

```python
import functools

import jax
import jax.numpy as jnp
from jax import lax
from jax.experimental import pallas as pl
from jax.experimental.pallas import tpu as pltpu
from jax.sharding import PartitionSpec as P

NZ, NY, NX = 8, 4, 4
BF16, F32 = jnp.bfloat16, jnp.float32
VMEM_LIMIT = 20 * 2**20
LIGHT = pl.CostEstimate(flops=1, bytes_accessed=1, transcendentals=0)
HEAVY = pl.CostEstimate(flops=4 * 512 * 768 * 5 * 384, bytes_accessed=5 * 2**22, transcendentals=0)


def along_z(value, step):
    moves = [(2 * z + c, 2 * ((z + step) % NZ) + c) for z in range(NZ) for c in range(2)]
    return lax.ppermute(value, "row", moves)


def along_x(value, step):
    moves = [(NX * y + x, NX * y + (x + step) % NX) for y in range(NY) for x in range(NX)]
    return lax.ppermute(value, "col", moves)


def along_y(value, step):
    moves = [(NX * y + x, NX * ((y + step) % NY) + x) for y in range(NY) for x in range(NX)]
    return lax.ppermute(value, "col", moves)


def to_sibling(value):
    return lax.ppermute(value, "row", [(i, i ^ 1) for i in range(2 * NZ)])


def after(value, earlier):
    return lax.optimization_barrier((value, earlier))[0]


def gelu_both(pre_act, grad_act):
    factor = 0.7978845608028654
    tangent = jnp.tanh(factor * (pre_act + 0.044715 * pre_act * pre_act * pre_act))
    activated = (0.5 * pre_act * (1.0 + tangent)).astype(BF16)
    derivative = 0.5 * (1.0 + tangent) + 0.5 * pre_act * (1.0 - tangent * tangent) * factor * (
        1.0 + 3.0 * 0.044715 * pre_act * pre_act
    )
    return activated, (grad_act * derivative).astype(BF16)


def dot(left, right):
    return jnp.dot(left, right, preferred_element_type=F32)


def dot_t(left, right):
    return lax.dot_general(left, right, (((1,), (1,)), ((), ())), preferred_element_type=F32)


FIRST, SECOND = (4, 3), (5, 2, 6, 1, 7, 0)
NEAR, FAR = (7, 1, 6, 2), (5, 3, 4, 0)


def pick(step, table):
    value = jnp.int32(table[0])
    for place, entry in enumerate(table):
        value = jnp.where(step == place, entry, value)
    return value


def next_pair(step, table, where_ref, w1_ref, w2_ref, w1_buf, w2_buf, sems):
    piece = w1_buf.shape[2] // 2

    def copies(at, slot, part):
        place = pl.ds(pl.multiple_of(at * piece, piece), piece)
        half = pl.ds(part * piece, piece)
        return (
            pltpu.make_async_copy(w1_ref.at[:, place], w1_buf.at[slot, :, half], sems.at[part, slot]),
            pltpu.make_async_copy(w2_ref.at[place, :], w2_buf.at[slot, half, :], sems.at[2 + part, slot]),
        )

    def start(pair):
        for part in range(2):
            at = lax.rem(where_ref[0] + pick(pair, table[part::2]), NZ)
            for copy in copies(at, lax.rem(pair, 3), part):
                copy.start()

    @pl.when(step == 0)
    def _():
        start(jnp.int32(0))
        if len(table) > 2:
            start(jnp.int32(1))

    @pl.when(step + 2 < len(table) // 2)
    def _():
        start(step + 2)

    slot = lax.rem(step, 3)
    for part in range(2):
        for copy in copies(0, slot, part):
            copy.wait()
    return slot


def weight_buffers(depth, piece):
    return [
        pltpu.VMEM((3, depth, 2 * piece), BF16),
        pltpu.VMEM((3, 2 * piece, depth), BF16),
        pltpu.SemaphoreType.DMA((4, 3)),
    ]


def hidden_kernel(table, where_ref, x_ref, w1_ref, w2_ref, mine_ref, other_ref, w1_buf, w2_buf, sems):
    slot = next_pair(pl.program_id(0), table, where_ref, w1_ref, w2_ref, w1_buf, w2_buf, sems)
    half, piece = mine_ref.shape[2:]
    for t, terms in enumerate((lambda: dot(x_ref[0], w1_buf[slot]), lambda: dot_t(x_ref[1], w2_buf[slot]))):
        value = terms()
        for part in range(2):
            columns = slice(part * piece, (part + 1) * piece)
            mine_ref[part, t] = value[:half, columns]
            other_ref[part, t] = value[half:, columns]


def call(kernel, name, table, where, operands, specs, w1, w2, out_shape, out_specs, **more):
    depth, piece = w1.shape[0], w1.shape[1] // NZ
    return pl.pallas_call(
        functools.partial(kernel, table),
        grid_spec=pltpu.PrefetchScalarGridSpec(
            num_scalar_prefetch=1,
            grid=(len(table) // 2,),
            in_specs=specs + [pl.BlockSpec(memory_space=pl.ANY)] * 2,
            out_specs=out_specs,
            scratch_shapes=weight_buffers(depth, piece),
        ),
        out_shape=out_shape,
        cost_estimate=HEAVY if table == SECOND else LIGHT,
        compiler_params=pltpu.CompilerParams(vmem_limit_bytes=VMEM_LIMIT),
        name=name,
        **more,
    )(where, *operands, w1, w2)


def touch_kernel(where_ref, w1_ref, w2_ref, out_ref):
    out_ref[0] = where_ref[0]


def touched(where, w1, w2):
    return pl.pallas_call(
        touch_kernel,
        in_specs=[pl.BlockSpec(memory_space=pltpu.SMEM)] + [pl.BlockSpec(memory_space=pl.ANY)] * 2,
        out_specs=pl.BlockSpec(memory_space=pltpu.SMEM),
        out_shape=jax.ShapeDtypeStruct((1,), jnp.int32),
        cost_estimate=pl.CostEstimate(flops=1, bytes_accessed=4 * w1.size, transcendentals=0),
        name="touched",
    )(where, w1, w2)


def whole(value):
    return pl.BlockSpec(value.shape, lambda j, where_ref: (0,) * len(value.shape))


def hidden_terms(name, table, where, tokens, w1, w2):
    half, piece = tokens.shape[1] // 2, w1.shape[1] // NZ
    out = jax.ShapeDtypeStruct((len(table), 2, half, piece), F32)
    block = pl.BlockSpec((2, 2, half, piece), lambda j, where_ref: (j, 0, 0, 0))
    mine, other = call(
        hidden_kernel, name, table, where, [tokens], [whole(tokens)], w1, w2, [out, out], [block, block]
    )
    return mine, other


def joined(t, left, right, left_sib, right_sib):
    mine = jnp.concatenate([left[t], right[t]], axis=1)
    other = jnp.concatenate([left_sib[t], right_sib[t]], axis=1)
    return jnp.concatenate([mine, other], axis=0)


def near_kernel(table, where_ref, mine_ref, other_ref, w1_ref, w2_ref, out_ref, w1_buf, w2_buf, sems):
    step = pl.program_id(0)
    slot = next_pair(step, table, where_ref, w1_ref, w2_ref, w1_buf, w2_buf, sems)
    parts = (mine_ref.at[0], mine_ref.at[1], other_ref.at[0], other_ref.at[1])

    @pl.when(step == 0)
    def _():
        out_ref[0] = dot(joined(0, *parts), w2_buf[slot])
        out_ref[1] = dot_t(joined(1, *parts), w1_buf[slot])

    @pl.when(step > 0)
    def _():
        out_ref[0] += dot(joined(0, *parts), w2_buf[slot])
        out_ref[1] += dot_t(joined(1, *parts), w1_buf[slot])


def far_kernel(
    table, where_ref, acc_ref, three_ref, three_sib_ref, four_ref, four_sib_ref, own_ref, own_sib_ref, w1_ref, w2_ref,
    out_ref, w1_buf, w2_buf, sems,
):
    step = pl.program_id(0)
    slot = next_pair(step, table, where_ref, w1_ref, w2_ref, w1_buf, w2_buf, sems)

    @pl.when(step == 0)
    def _():
        parts = (three_ref.at[0], three_ref.at[1], three_sib_ref.at[0], three_sib_ref.at[1])
        out_ref[0] = acc_ref[0] + dot(joined(0, *parts), w2_buf[slot])
        out_ref[1] = acc_ref[1] + dot_t(joined(1, *parts), w1_buf[slot])

    @pl.when(step == 1)
    def _():
        parts = (four_ref, own_ref, four_sib_ref, own_sib_ref)
        out_ref[0] += dot(joined(0, *parts), w2_buf[slot])
        out_ref[1] += dot_t(joined(1, *parts), w1_buf[slot])


def summed_over_z(where, tokens, w1, w2):
    mine, other = hidden_terms("first_terms", FIRST, where, tokens, w1, w2)
    sib = to_sibling(other)
    mine2, other2 = hidden_terms("second_terms", SECOND, where, after(tokens, other), w1, w2)
    sib2 = to_sibling(after(other2, sib))

    def total(j):
        if j in FIRST:
            return mine[FIRST.index(j)] + sib[FIRST.index(j)]
        return mine2[SECOND.index(j)] + sib2[SECOND.index(j)]

    quarter = mine.shape[2] // 2
    start = total(4).astype(BF16)
    up, down = along_z(start[:, :quarter], 1).astype(F32), along_z(start[:, quarter:], -1).astype(F32)
    blank = jnp.zeros_like(up)
    up, down = jnp.concatenate([up, blank], axis=1), jnp.concatenate([blank, down], axis=1)
    for far in (3, 2, 1):
        up = along_z((up + total(far)).astype(BF16), 1).astype(F32)
        down = along_z((down + total(NZ - far)).astype(BF16), -1).astype(F32)
    return total(0) + (up + down)


def output_terms(where, own, w1, w2):
    quarter = own.shape[1] // 2
    depth = w1.shape[0]
    ups, downs = [own], [own]
    for _ in range(3):
        ups.append(along_z(ups[-1], 1))
        downs.append(along_z(downs[-1], -1))
    own_sib = to_sibling(own)
    near = jnp.stack([ups[1], downs[1], ups[2], downs[2]])
    near_sib = to_sibling(near)
    three = jnp.stack([ups[3], downs[3]])
    three_sib = to_sibling(three)
    four = along_z(ups[3][:, :quarter], 1), along_z(downs[3][:, quarter:], -1)

    out = jax.ShapeDtypeStruct((2, 2 * own.shape[1], depth), F32)
    block = pl.BlockSpec((2, *own.shape), lambda j, where_ref: (j, 0, 0, 0))
    acc = call(near_kernel, "near_terms", NEAR, where, [near, near_sib], [block, block], w1, w2, out, whole(out))
    four = jnp.concatenate(after(four, acc), axis=1)
    four_sib = to_sibling(four)
    operands = [acc, three, three_sib, four, four_sib, own, own_sib]
    return call(
        far_kernel, "far_terms", FAR, where, operands, [whole(value) for value in operands], w1, w2, out, whole(out),
        input_output_aliases={1: 0},
    )


def per_device(inputs, w1, w2, cotangent):
    row = lax.axis_index("row")
    first = row % 2 == 0
    where = touched((row // 2).astype(jnp.int32).reshape(1), w1, w2)
    block, depth = inputs.shape

    def ordered(by_x, axis):
        low, high = jnp.stack(by_x[:2], axis=axis), jnp.stack(by_x[2:], axis=axis)
        return jnp.where(first, low, high), jnp.where(first, high, low)

    by_x = [inputs] + [along_x(inputs, -r) for r in (1, 2, 3)]
    by_y = [cotangent] + [along_y(cotangent, -k) for k in (1, 2, 3)]
    here = jnp.stack(ordered(by_x, 0))
    column = jnp.stack(by_y)
    forward = jnp.stack([here] + [along_y(here, -k) for k in (1, 2, 3)], axis=1)
    backward = jnp.stack(ordered([column] + [along_x(column, -r) for r in (1, 2, 3)], 1))
    tokens = jnp.stack([forward, backward]).reshape(2, NY * NX * block, depth)

    both = summed_over_z(where, tokens, w1, w2)
    out = output_terms(where, jnp.stack(gelu_both(both[0], both[1])), w1, w2)
    out = out.reshape(2, 2, NY, 2, block, depth)

    def by_distance(halves, axis):
        low, high = jnp.where(first, halves[0], halves[1]), jnp.where(first, halves[1], halves[0])
        return [lax.index_in_dim(part, r, axis, keepdims=False) for part in (low, high) for r in range(2)]

    def summed(parts, along, kind):
        total = parts[0]
        for distance in (2, 1, 3):
            total = total + along(parts[distance].astype(kind), distance).astype(F32)
        return total

    forward = summed([out[0, :, k] for k in range(NY)], along_y, BF16)
    backward = summed(by_distance(out[1], 1), along_x, BF16)
    forward = summed(by_distance(forward, 0), along_x, F32)
    backward = summed([backward[k] for k in range(NY)], along_y, F32)
    return forward.astype(BF16), backward.astype(BF16)


def solution(mesh):
    return jax.shard_map(
        per_device,
        mesh=mesh,
        in_specs=(P("col", "row"), P("row", "col"), P("col", "row"), P("col", "row")),
        out_specs=(P("col", "row"), P("col", "row")),
        check_vma=False,
    )
```

```python
import functools

import jax
import jax.numpy as jnp
from jax import lax
from jax.experimental import pallas as pl
from jax.experimental.pallas import tpu as pltpu
from jax.sharding import PartitionSpec as P

NZ, NY, NX = 8, 4, 4
BF16, F32 = jnp.bfloat16, jnp.float32
VMEM_LIMIT = 20 * 2**20
LIGHT = pl.CostEstimate(flops=1, bytes_accessed=1, transcendentals=0)
HEAVY = pl.CostEstimate(flops=4 * 512 * 768 * 4 * 384, bytes_accessed=2**24, transcendentals=0)


def along_z(value, step):
    moves = [(2 * z + c, 2 * ((z + step) % NZ) + c) for z in range(NZ) for c in range(2)]
    return lax.ppermute(value, "row", moves)


def along_x(value, step):
    moves = [(NX * y + x, NX * y + (x + step) % NX) for y in range(NY) for x in range(NX)]
    return lax.ppermute(value, "col", moves)


def along_y(value, step):
    moves = [(NX * y + x, NX * ((y + step) % NY) + x) for y in range(NY) for x in range(NX)]
    return lax.ppermute(value, "col", moves)


def to_sibling(value):
    return lax.ppermute(value, "row", [(i, i ^ 1) for i in range(2 * NZ)])


def after(value, earlier):
    return lax.optimization_barrier((value, earlier))[0]


def gelu_both(pre_act, grad_act):
    factor = 0.7978845608028654
    tangent = jnp.tanh(factor * (pre_act + 0.044715 * pre_act * pre_act * pre_act))
    activated = (0.5 * pre_act * (1.0 + tangent)).astype(BF16)
    derivative = 0.5 * (1.0 + tangent) + 0.5 * pre_act * (1.0 - tangent * tangent) * factor * (
        1.0 + 3.0 * 0.044715 * pre_act * pre_act
    )
    return activated, (grad_act * derivative).astype(BF16)


def dot(left, right):
    return jnp.dot(left, right, preferred_element_type=F32)


def dot_t(left, right):
    return lax.dot_general(left, right, (((1,), (1,)), ((), ())), preferred_element_type=F32)


FIRST, SECOND, THIRD = (4, 3), (5, 2, 6, 1), (7, 0)
NEAR, MIDDLE, FAR = (7, 1, 6, 2), (5, 3), (4, 0)


def pick(step, table):
    value = jnp.int32(table[0])
    for place, entry in enumerate(table):
        value = jnp.where(step == place, entry, value)
    return value


def next_pair(step, table, where_ref, w1_ref, w2_ref, w1_buf, w2_buf, sems):
    piece = w1_buf.shape[2] // 2

    def copies(at, slot, part):
        place = pl.ds(pl.multiple_of(at * piece, piece), piece)
        half = pl.ds(part * piece, piece)
        return (
            pltpu.make_async_copy(w1_ref.at[:, place], w1_buf.at[slot, :, half], sems.at[part, slot]),
            pltpu.make_async_copy(w2_ref.at[place, :], w2_buf.at[slot, half, :], sems.at[2 + part, slot]),
        )

    def start(pair):
        for part in range(2):
            at = lax.rem(where_ref[0] + pick(pair, table[part::2]), NZ)
            for copy in copies(at, lax.rem(pair, 3), part):
                copy.start()

    @pl.when(step == 0)
    def _():
        start(jnp.int32(0))
        if len(table) > 2:
            start(jnp.int32(1))

    @pl.when(step + 2 < len(table) // 2)
    def _():
        start(step + 2)

    slot = lax.rem(step, 3)
    for part in range(2):
        for copy in copies(0, slot, part):
            copy.wait()
    return slot


def weight_buffers(depth, piece):
    return [
        pltpu.VMEM((3, depth, 2 * piece), BF16),
        pltpu.VMEM((3, 2 * piece, depth), BF16),
        pltpu.SemaphoreType.DMA((4, 3)),
    ]


def hidden_kernel(table, where_ref, x_ref, w1_ref, w2_ref, mine_ref, other_ref, w1_buf, w2_buf, sems):
    slot = next_pair(pl.program_id(0), table, where_ref, w1_ref, w2_ref, w1_buf, w2_buf, sems)
    half, piece = mine_ref.shape[2:]
    for t, terms in enumerate((lambda: dot(x_ref[0], w1_buf[slot]), lambda: dot_t(x_ref[1], w2_buf[slot]))):
        value = terms()
        for part in range(2):
            columns = slice(part * piece, (part + 1) * piece)
            mine_ref[part, t] = value[:half, columns]
            other_ref[part, t] = value[half:, columns]


def call(kernel, name, table, where, operands, specs, w1, w2, out_shape, out_specs, **more):
    depth, piece = w1.shape[0], w1.shape[1] // NZ
    return pl.pallas_call(
        functools.partial(kernel, table),
        grid_spec=pltpu.PrefetchScalarGridSpec(
            num_scalar_prefetch=1,
            grid=(len(table) // 2,),
            in_specs=specs + [pl.BlockSpec(memory_space=pl.ANY)] * 2,
            out_specs=out_specs,
            scratch_shapes=weight_buffers(depth, piece),
        ),
        out_shape=out_shape,
        cost_estimate=HEAVY if table in (SECOND, THIRD, NEAR, MIDDLE) else LIGHT,
        compiler_params=pltpu.CompilerParams(vmem_limit_bytes=VMEM_LIMIT),
        name=name,
        **more,
    )(where, *operands, w1, w2)


def touch_kernel(where_ref, w1_ref, w2_ref, out_ref):
    out_ref[0] = where_ref[0]


def touched(where, w1, w2):
    return pl.pallas_call(
        touch_kernel,
        in_specs=[pl.BlockSpec(memory_space=pltpu.SMEM)] + [pl.BlockSpec(memory_space=pl.ANY)] * 2,
        out_specs=pl.BlockSpec(memory_space=pltpu.SMEM),
        out_shape=jax.ShapeDtypeStruct((1,), jnp.int32),
        cost_estimate=pl.CostEstimate(flops=1, bytes_accessed=4 * w1.size, transcendentals=0),
        name="touched",
    )(where, w1, w2)


def whole(value):
    return pl.BlockSpec(value.shape, lambda j, where_ref: (0,) * len(value.shape))


def hidden_terms(name, table, where, tokens, w1, w2):
    half, piece = tokens.shape[1] // 2, w1.shape[1] // NZ
    out = jax.ShapeDtypeStruct((len(table), 2, half, piece), F32)
    block = pl.BlockSpec((2, 2, half, piece), lambda j, where_ref: (j, 0, 0, 0))
    mine, other = call(
        hidden_kernel, name, table, where, [tokens], [whole(tokens)], w1, w2, [out, out], [block, block]
    )
    return mine, other


def joined(t, left, right, left_sib, right_sib):
    mine = jnp.concatenate([left[t], right[t]], axis=1)
    other = jnp.concatenate([left_sib[t], right_sib[t]], axis=1)
    return jnp.concatenate([mine, other], axis=0)


def near_kernel(table, where_ref, mine_ref, other_ref, w1_ref, w2_ref, out_ref, w1_buf, w2_buf, sems):
    step = pl.program_id(0)
    slot = next_pair(step, table, where_ref, w1_ref, w2_ref, w1_buf, w2_buf, sems)
    parts = (mine_ref.at[0], mine_ref.at[1], other_ref.at[0], other_ref.at[1])

    @pl.when(step == 0)
    def _():
        out_ref[0] = dot(joined(0, *parts), w2_buf[slot])
        out_ref[1] = dot_t(joined(1, *parts), w1_buf[slot])

    @pl.when(step > 0)
    def _():
        out_ref[0] += dot(joined(0, *parts), w2_buf[slot])
        out_ref[1] += dot_t(joined(1, *parts), w1_buf[slot])


def more_kernel(
    table, where_ref, acc_ref, left_ref, right_ref, left_sib_ref, right_sib_ref, w1_ref, w2_ref, out_ref, w1_buf, w2_buf, sems
):
    slot = next_pair(pl.program_id(0), table, where_ref, w1_ref, w2_ref, w1_buf, w2_buf, sems)
    parts = (left_ref, right_ref, left_sib_ref, right_sib_ref)
    out_ref[0] = acc_ref[0] + dot(joined(0, *parts), w2_buf[slot])
    out_ref[1] = acc_ref[1] + dot_t(joined(1, *parts), w1_buf[slot])


def summed_over_z(where, tokens, w1, w2):
    mine, sib = {}, {}

    def work_on(name, table, earlier):
        kept, sent = hidden_terms(name, table, where, after(tokens, earlier), w1, w2)
        mine.update({j: kept[i] for i, j in enumerate(table)})
        return sent

    def exchange(table, sent):
        got = to_sibling(sent)
        sib.update({j: got[i] for i, j in enumerate(table)})
        return got

    def total(j):
        return mine[j] + sib[j]

    sent1 = work_on("first_terms", FIRST, where)
    got1 = exchange(FIRST, sent1)
    sent2 = work_on("second_terms", SECOND, sent1)
    got2 = exchange(SECOND, after(sent2, got1))
    start = total(4).astype(BF16)
    sent3 = work_on("third_terms", THIRD, (start, sent2))
    exchange(THIRD, after(sent3, got2))

    quarter = start.shape[1] // 2
    up, down = along_z(start[:, :quarter], 1).astype(F32), along_z(start[:, quarter:], -1).astype(F32)
    blank = jnp.zeros_like(up)
    up, down = jnp.concatenate([up, blank], axis=1), jnp.concatenate([blank, down], axis=1)
    for far in (3, 2, 1):
        up = along_z((up + total(far)).astype(BF16), 1).astype(F32)
        down = along_z((down + total(NZ - far)).astype(BF16), -1).astype(F32)
    return total(0) + (up + down)


def output_terms(where, own, w1, w2):
    quarter = own.shape[1] // 2
    depth = w1.shape[0]
    ups, downs = [own], [own]
    own_sib = to_sibling(own)
    for _ in range(2):
        ups.append(along_z(ups[-1], 1))
        downs.append(along_z(downs[-1], -1))
    near = jnp.stack([ups[1], downs[1], ups[2], downs[2]])
    near_sib = to_sibling(near)
    out = jax.ShapeDtypeStruct((2, 2 * own.shape[1], depth), F32)
    block = pl.BlockSpec((2, *own.shape), lambda j, where_ref: (j, 0, 0, 0))
    acc = call(near_kernel, "near_terms", NEAR, where, [near, near_sib], [block, block], w1, w2, out, whole(out))

    def more(name, table, operands):
        specs = [whole(value) for value in operands]
        return call(
            more_kernel, name, table, where, operands, specs, w1, w2, out, whole(out), input_output_aliases={1: 0}
        )

    three = after((along_z(ups[2], 1), along_z(downs[2], -1)), acc)
    three_sib = to_sibling(jnp.stack(three))
    four = along_z(three[0][:, :quarter], 1), along_z(three[1][:, quarter:], -1)
    acc = more("middle_terms", MIDDLE, [acc, *three, three_sib[0], three_sib[1]])
    four = jnp.concatenate(after(four, acc), axis=1)
    return more("far_terms", FAR, [acc, four, own, to_sibling(four), own_sib])


def per_device(inputs, w1, w2, cotangent):
    row = lax.axis_index("row")
    first = row % 2 == 0
    where = touched((row // 2).astype(jnp.int32).reshape(1), w1, w2)
    block, depth = inputs.shape

    def ordered(by_x, axis):
        low, high = jnp.stack(by_x[:2], axis=axis), jnp.stack(by_x[2:], axis=axis)
        return jnp.where(first, low, high), jnp.where(first, high, low)

    by_x = [inputs] + [along_x(inputs, -r) for r in (1, 2, 3)]
    by_y = [cotangent] + [along_y(cotangent, -k) for k in (1, 2, 3)]
    here = jnp.stack(ordered(by_x, 0))
    column = jnp.stack(by_y)
    forward = jnp.stack([here] + [along_y(here, -k) for k in (1, 2, 3)], axis=1)
    backward = jnp.stack(ordered([column] + [along_x(column, -r) for r in (1, 2, 3)], 1))
    tokens = jnp.stack([forward, backward]).reshape(2, NY * NX * block, depth)

    both = summed_over_z(where, tokens, w1, w2)
    out = output_terms(where, jnp.stack(gelu_both(both[0], both[1])), w1, w2)
    out = out.reshape(2, 2, NY, 2, block, depth)

    def by_distance(halves, axis):
        low, high = jnp.where(first, halves[0], halves[1]), jnp.where(first, halves[1], halves[0])
        return [lax.index_in_dim(part, r, axis, keepdims=False) for part in (low, high) for r in range(2)]

    def summed(parts, along, kind):
        total = parts[0]
        for distance in (2, 1, 3):
            total = total + along(parts[distance].astype(kind), distance).astype(F32)
        return total

    forward = summed([out[0, :, k] for k in range(NY)], along_y, BF16)
    backward = summed(by_distance(out[1], 1), along_x, BF16)
    forward = summed(by_distance(forward, 0), along_x, F32)
    backward = summed([backward[k] for k in range(NY)], along_y, F32)
    return forward.astype(BF16), backward.astype(BF16)


def solution(mesh):
    return jax.shard_map(
        per_device,
        mesh=mesh,
        in_specs=(P("col", "row"), P("row", "col"), P("col", "row"), P("col", "row")),
        out_specs=(P("col", "row"), P("col", "row")),
        check_vma=False,
    )
```

```python
import functools

import jax
import jax.numpy as jnp
from jax import lax
from jax.experimental import pallas as pl
from jax.experimental.pallas import tpu as pltpu
from jax.sharding import PartitionSpec as P

NZ, NY, NX = 8, 4, 4
BF16, F32 = jnp.bfloat16, jnp.float32
VMEM_LIMIT = 20 * 2**20
LIGHT = pl.CostEstimate(flops=1, bytes_accessed=1, transcendentals=0)
HEAVY = pl.CostEstimate(flops=4 * 512 * 768 * 5 * 384, bytes_accessed=5 * 2**22, transcendentals=0)


def along_z(value, step):
    moves = [(2 * z + c, 2 * ((z + step) % NZ) + c) for z in range(NZ) for c in range(2)]
    return lax.ppermute(value, "row", moves)


def along_x(value, step):
    moves = [(NX * y + x, NX * y + (x + step) % NX) for y in range(NY) for x in range(NX)]
    return lax.ppermute(value, "col", moves)


def along_y(value, step):
    moves = [(NX * y + x, NX * ((y + step) % NY) + x) for y in range(NY) for x in range(NX)]
    return lax.ppermute(value, "col", moves)


def to_sibling(value):
    return lax.ppermute(value, "row", [(i, i ^ 1) for i in range(2 * NZ)])


def after(value, earlier):
    return lax.optimization_barrier((value, earlier))[0]


def gelu_both(pre_act, grad_act):
    factor = 0.7978845608028654
    tangent = jnp.tanh(factor * (pre_act + 0.044715 * pre_act * pre_act * pre_act))
    activated = (0.5 * pre_act * (1.0 + tangent)).astype(BF16)
    derivative = 0.5 * (1.0 + tangent) + 0.5 * pre_act * (1.0 - tangent * tangent) * factor * (
        1.0 + 3.0 * 0.044715 * pre_act * pre_act
    )
    return activated, (grad_act * derivative).astype(BF16)


def dot(left, right):
    return jnp.dot(left, right, preferred_element_type=F32)


def dot_t(left, right):
    return lax.dot_general(left, right, (((1,), (1,)), ((), ())), preferred_element_type=F32)


FIRST, SECOND = (4, 3), (5, 2, 6, 1, 7, 0)
NEAR, FAR = (7, 1, 6, 2), (5, 3, 4, 0)


def pick(step, table):
    value = jnp.int32(table[0])
    for place, entry in enumerate(table):
        value = jnp.where(step == place, entry, value)
    return value


def next_pair(step, table, where_ref, w1_ref, w2_ref, w1_buf, w2_buf, sems):
    piece = w1_buf.shape[2] // 2

    def copies(at, slot, part):
        place = pl.ds(pl.multiple_of(at * piece, piece), piece)
        half = pl.ds(part * piece, piece)
        return (
            pltpu.make_async_copy(w1_ref.at[:, place], w1_buf.at[slot, :, half], sems.at[part, slot]),
            pltpu.make_async_copy(w2_ref.at[place, :], w2_buf.at[slot, half, :], sems.at[2 + part, slot]),
        )

    def start(pair):
        for part in range(2):
            at = lax.rem(where_ref[0] + pick(pair, table[part::2]), NZ)
            for copy in copies(at, lax.rem(pair, 3), part):
                copy.start()

    @pl.when(step == 0)
    def _():
        start(jnp.int32(0))
        if len(table) > 2:
            start(jnp.int32(1))

    @pl.when(step + 2 < len(table) // 2)
    def _():
        start(step + 2)

    slot = lax.rem(step, 3)
    for part in range(2):
        for copy in copies(0, slot, part):
            copy.wait()
    return slot


def weight_buffers(depth, piece):
    return [
        pltpu.VMEM((3, depth, 2 * piece), BF16),
        pltpu.VMEM((3, 2 * piece, depth), BF16),
        pltpu.SemaphoreType.DMA((4, 3)),
    ]


def hidden_kernel(table, where_ref, x_ref, w1_ref, w2_ref, mine_ref, other_ref, w1_buf, w2_buf, sems):
    slot = next_pair(pl.program_id(0), table, where_ref, w1_ref, w2_ref, w1_buf, w2_buf, sems)
    half, piece = mine_ref.shape[2:]
    for t, terms in enumerate((lambda: dot(x_ref[0], w1_buf[slot]), lambda: dot_t(x_ref[1], w2_buf[slot]))):
        value = terms()
        for part in range(2):
            columns = slice(part * piece, (part + 1) * piece)
            mine_ref[part, t] = value[:half, columns]
            other_ref[part, t] = value[half:, columns]


def call(kernel, name, table, where, operands, specs, w1, w2, out_shape, out_specs, **more):
    depth, piece = w1.shape[0], w1.shape[1] // NZ
    return pl.pallas_call(
        functools.partial(kernel, table),
        grid_spec=pltpu.PrefetchScalarGridSpec(
            num_scalar_prefetch=1,
            grid=(len(table) // 2,),
            in_specs=specs + [pl.BlockSpec(memory_space=pl.ANY)] * 2,
            out_specs=out_specs,
            scratch_shapes=weight_buffers(depth, piece),
        ),
        out_shape=out_shape,
        cost_estimate=HEAVY if table == SECOND else LIGHT,
        compiler_params=pltpu.CompilerParams(vmem_limit_bytes=VMEM_LIMIT),
        name=name,
        **more,
    )(where, *operands, w1, w2)


def touch_kernel(where_ref, weight_ref, out_ref):
    out_ref[0] = where_ref[0]


def touched(where, weight):
    return pl.pallas_call(
        touch_kernel,
        in_specs=[pl.BlockSpec(memory_space=pltpu.SMEM), pl.BlockSpec(memory_space=pl.ANY)],
        out_specs=pl.BlockSpec(memory_space=pltpu.SMEM),
        out_shape=jax.ShapeDtypeStruct((1,), jnp.int32),
        cost_estimate=pl.CostEstimate(flops=1, bytes_accessed=2 * weight.size, transcendentals=0),
        name="touched",
    )(where, weight)


def whole(value):
    return pl.BlockSpec(value.shape, lambda j, where_ref: (0,) * len(value.shape))


def hidden_terms(name, table, where, tokens, w1, w2):
    half, piece = tokens.shape[1] // 2, w1.shape[1] // NZ
    out = jax.ShapeDtypeStruct((len(table), 2, half, piece), F32)
    block = pl.BlockSpec((2, 2, half, piece), lambda j, where_ref: (j, 0, 0, 0))
    mine, other = call(
        hidden_kernel, name, table, where, [tokens], [whole(tokens)], w1, w2, [out, out], [block, block]
    )
    return mine, other


def joined(t, left, right, left_sib, right_sib):
    mine = jnp.concatenate([left[t], right[t]], axis=1)
    other = jnp.concatenate([left_sib[t], right_sib[t]], axis=1)
    return jnp.concatenate([mine, other], axis=0)


def near_kernel(
    table, where_ref, one_ref, two_ref, one_sib_ref, two_sib_ref, w1_ref, w2_ref, out_ref, w1_buf, w2_buf, sems
):
    step = pl.program_id(0)
    slot = next_pair(step, table, where_ref, w1_ref, w2_ref, w1_buf, w2_buf, sems)

    @pl.when(step == 0)
    def _():
        parts = (one_ref.at[0], one_ref.at[1], one_sib_ref.at[0], one_sib_ref.at[1])
        out_ref[0] = dot(joined(0, *parts), w2_buf[slot])
        out_ref[1] = dot_t(joined(1, *parts), w1_buf[slot])

    @pl.when(step == 1)
    def _():
        parts = (two_ref.at[0], two_ref.at[1], two_sib_ref.at[0], two_sib_ref.at[1])
        out_ref[0] += dot(joined(0, *parts), w2_buf[slot])
        out_ref[1] += dot_t(joined(1, *parts), w1_buf[slot])


def far_kernel(
    table, where_ref, acc_ref, three_ref, three_sib_ref, four_ref, four_sib_ref, own_ref, own_sib_ref, w1_ref, w2_ref,
    out_ref, w1_buf, w2_buf, sems,
):
    step = pl.program_id(0)
    slot = next_pair(step, table, where_ref, w1_ref, w2_ref, w1_buf, w2_buf, sems)

    @pl.when(step == 0)
    def _():
        parts = (three_ref.at[0], three_ref.at[1], three_sib_ref.at[0], three_sib_ref.at[1])
        out_ref[0] = acc_ref[0] + dot(joined(0, *parts), w2_buf[slot])
        out_ref[1] = acc_ref[1] + dot_t(joined(1, *parts), w1_buf[slot])

    @pl.when(step == 1)
    def _():
        parts = (four_ref, own_ref, four_sib_ref, own_sib_ref)
        out_ref[0] += dot(joined(0, *parts), w2_buf[slot])
        out_ref[1] += dot_t(joined(1, *parts), w1_buf[slot])


def summed_over_z(where, tokens, w1, w2):
    mine, other = hidden_terms("first_terms", FIRST, where, tokens, w1, w2)
    sib = to_sibling(other)
    mine2, other2 = hidden_terms("second_terms", SECOND, where, after(tokens, other), w1, w2)
    sib2 = to_sibling(after(other2, sib))

    def total(j):
        if j in FIRST:
            return mine[FIRST.index(j)] + sib[FIRST.index(j)]
        return mine2[SECOND.index(j)] + sib2[SECOND.index(j)]

    quarter = mine.shape[2] // 2
    start = total(4).astype(BF16)
    up, down = along_z(start[:, :quarter], 1).astype(F32), along_z(start[:, quarter:], -1).astype(F32)
    blank = jnp.zeros_like(up)
    up, down = jnp.concatenate([up, blank], axis=1), jnp.concatenate([blank, down], axis=1)
    for far in (3, 2, 1):
        up = along_z((up + total(far)).astype(BF16), 1).astype(F32)
        down = along_z((down + total(NZ - far)).astype(BF16), -1).astype(F32)
    return total(0) + (up + down)


def output_terms(where, own, w1, w2):
    quarter = own.shape[1] // 2
    depth = w1.shape[0]
    ups, downs = [own], [own]
    for _ in range(3):
        ups.append(along_z(ups[-1], 1))
        downs.append(along_z(downs[-1], -1))
    own_sib = to_sibling(own)
    one, two = jnp.stack([ups[1], downs[1]]), jnp.stack([ups[2], downs[2]])
    near = [one, two, to_sibling(one), to_sibling(two)]
    three = jnp.stack([ups[3], downs[3]])
    three_sib = to_sibling(three)
    four = along_z(ups[3][:, :quarter], 1), along_z(downs[3][:, quarter:], -1)

    out = jax.ShapeDtypeStruct((2, 2 * own.shape[1], depth), F32)
    specs = [whole(value) for value in near]
    acc = call(near_kernel, "near_terms", NEAR, where, near, specs, w1, w2, out, whole(out))
    four = jnp.concatenate(after(four, acc), axis=1)
    four_sib = to_sibling(four)
    operands = [acc, three, three_sib, four, four_sib, own, own_sib]
    return call(
        far_kernel, "far_terms", FAR, where, operands, [whole(value) for value in operands], w1, w2, out, whole(out),
        input_output_aliases={1: 0},
    )


def per_device(inputs, w1, w2, cotangent):
    row = lax.axis_index("row")
    first = row % 2 == 0
    where = touched(touched((row // 2).astype(jnp.int32).reshape(1), w2), w1)
    block, depth = inputs.shape

    def ordered(by_x, axis):
        low, high = jnp.stack(by_x[:2], axis=axis), jnp.stack(by_x[2:], axis=axis)
        return jnp.where(first, low, high), jnp.where(first, high, low)

    by_x = [inputs] + [along_x(inputs, -r) for r in (1, 2, 3)]
    by_y = [cotangent] + [along_y(cotangent, -k) for k in (1, 2, 3)]
    by_x, by_y = lax.optimization_barrier((by_x, by_y))
    here = jnp.stack(ordered(by_x, 0))
    column = jnp.stack(by_y)
    forward = jnp.stack([here] + [along_y(here, -k) for k in (1, 2, 3)], axis=1)
    backward = jnp.stack(ordered([column] + [along_x(column, -r) for r in (1, 2, 3)], 1))
    tokens = jnp.stack([forward, backward]).reshape(2, NY * NX * block, depth)

    both = summed_over_z(where, tokens, w1, w2)
    out = output_terms(where, jnp.stack(gelu_both(both[0], both[1])), w1, w2)
    out = out.reshape(2, 2, NY, 2, block, depth)

    def by_distance(halves, axis):
        low, high = jnp.where(first, halves[0], halves[1]), jnp.where(first, halves[1], halves[0])
        return [lax.index_in_dim(part, r, axis, keepdims=False) for part in (low, high) for r in range(2)]

    def summed(parts, along, kind):
        total = parts[0]
        for distance in (2, 1, 3):
            total = total + along(parts[distance].astype(kind), distance).astype(F32)
        return total

    forward = summed([out[0, :, k] for k in range(NY)], along_y, BF16)
    backward = summed(by_distance(out[1], 1), along_x, BF16)
    forward = summed(by_distance(forward, 0), along_x, F32)
    backward = summed([backward[k] for k in range(NY)], along_y, F32)
    return forward.astype(BF16), backward.astype(BF16)


def solution(mesh):
    return jax.shard_map(
        per_device,
        mesh=mesh,
        in_specs=(P("col", "row"), P("row", "col"), P("col", "row"), P("col", "row")),
        out_specs=(P("col", "row"), P("col", "row")),
        check_vma=False,
    )
```

```python
import functools

import jax
import jax.numpy as jnp
from jax import lax
from jax.experimental import pallas as pl
from jax.experimental.pallas import tpu as pltpu
from jax.sharding import PartitionSpec as P

NZ, NY, NX = 8, 4, 4
BF16, F32 = jnp.bfloat16, jnp.float32
VMEM_LIMIT = 20 * 2**20
LIGHT = pl.CostEstimate(flops=1, bytes_accessed=1, transcendentals=0)
HEAVY = pl.CostEstimate(flops=4 * 512 * 768 * 5 * 384, bytes_accessed=5 * 2**22, transcendentals=0)


def along_z(value, step):
    moves = [(2 * z + c, 2 * ((z + step) % NZ) + c) for z in range(NZ) for c in range(2)]
    return lax.ppermute(value, "row", moves)


def along_x(value, step):
    moves = [(NX * y + x, NX * y + (x + step) % NX) for y in range(NY) for x in range(NX)]
    return lax.ppermute(value, "col", moves)


def along_y(value, step):
    moves = [(NX * y + x, NX * ((y + step) % NY) + x) for y in range(NY) for x in range(NX)]
    return lax.ppermute(value, "col", moves)


def to_sibling(value):
    return lax.ppermute(value, "row", [(i, i ^ 1) for i in range(2 * NZ)])


def after(value, earlier):
    return lax.optimization_barrier((value, earlier))[0]


def gelu_both(pre_act, grad_act):
    factor = 0.7978845608028654
    tangent = jnp.tanh(factor * (pre_act + 0.044715 * pre_act * pre_act * pre_act))
    activated = (0.5 * pre_act * (1.0 + tangent)).astype(BF16)
    derivative = 0.5 * (1.0 + tangent) + 0.5 * pre_act * (1.0 - tangent * tangent) * factor * (
        1.0 + 3.0 * 0.044715 * pre_act * pre_act
    )
    return activated, (grad_act * derivative).astype(BF16)


def dot(left, right):
    return jnp.dot(left, right, preferred_element_type=F32)


def dot_t(left, right):
    return lax.dot_general(left, right, (((1,), (1,)), ((), ())), preferred_element_type=F32)


FIRST, SECOND = (4, 3), (5, 2, 6, 1, 7, 0)
NEAR, FAR = (7, 1, 6, 2), (5, 3, 4, 0)


def pick(step, table):
    value = jnp.int32(table[0])
    for place, entry in enumerate(table):
        value = jnp.where(step == place, entry, value)
    return value


def next_pair(step, table, where_ref, w1_ref, w2_ref, w1_buf, w2_buf, sems):
    piece = w1_buf.shape[2] // 2

    def copies(at, slot, part):
        place = pl.ds(pl.multiple_of(at * piece, piece), piece)
        half = pl.ds(part * piece, piece)
        return (
            pltpu.make_async_copy(w1_ref.at[:, place], w1_buf.at[slot, :, half], sems.at[part, slot]),
            pltpu.make_async_copy(w2_ref.at[place, :], w2_buf.at[slot, half, :], sems.at[2 + part, slot]),
        )

    def start(pair):
        for part in range(2):
            at = lax.rem(where_ref[0] + pick(pair, table[part::2]), NZ)
            for copy in copies(at, lax.rem(pair, 3), part):
                copy.start()

    @pl.when(step == 0)
    def _():
        start(jnp.int32(0))
        if len(table) > 2:
            start(jnp.int32(1))

    @pl.when(step + 2 < len(table) // 2)
    def _():
        start(step + 2)

    slot = lax.rem(step, 3)
    for part in range(2):
        for copy in copies(0, slot, part):
            copy.wait()
    return slot


def weight_buffers(depth, piece):
    return [
        pltpu.VMEM((3, depth, 2 * piece), BF16),
        pltpu.VMEM((3, 2 * piece, depth), BF16),
        pltpu.SemaphoreType.DMA((4, 3)),
    ]


def hidden_kernel(table, where_ref, x_ref, w1_ref, w2_ref, mine_ref, other_ref, w1_buf, w2_buf, sems):
    slot = next_pair(pl.program_id(0), table, where_ref, w1_ref, w2_ref, w1_buf, w2_buf, sems)
    half, piece = mine_ref.shape[2:]
    for t, terms in enumerate((lambda: dot(x_ref[0], w1_buf[slot]), lambda: dot_t(x_ref[1], w2_buf[slot]))):
        value = terms()
        for part in range(2):
            columns = slice(part * piece, (part + 1) * piece)
            mine_ref[part, t] = value[:half, columns]
            other_ref[part, t] = value[half:, columns]


def call(kernel, name, table, where, operands, specs, w1, w2, out_shape, out_specs, **more):
    depth, piece = w1.shape[0], w1.shape[1] // NZ
    return pl.pallas_call(
        functools.partial(kernel, table),
        grid_spec=pltpu.PrefetchScalarGridSpec(
            num_scalar_prefetch=1,
            grid=(len(table) // 2,),
            in_specs=specs + [pl.BlockSpec(memory_space=pl.ANY)] * 2,
            out_specs=out_specs,
            scratch_shapes=weight_buffers(depth, piece),
        ),
        out_shape=out_shape,
        cost_estimate=HEAVY if table == SECOND else LIGHT,
        compiler_params=pltpu.CompilerParams(vmem_limit_bytes=VMEM_LIMIT),
        name=name,
        **more,
    )(where, *operands, w1, w2)


def touch_kernel(where_ref, weight_ref, out_ref):
    out_ref[0] = where_ref[0]


def touched(where, weight):
    return pl.pallas_call(
        touch_kernel,
        in_specs=[pl.BlockSpec(memory_space=pltpu.SMEM), pl.BlockSpec(memory_space=pl.ANY)],
        out_specs=pl.BlockSpec(memory_space=pltpu.SMEM),
        out_shape=jax.ShapeDtypeStruct((1,), jnp.int32),
        cost_estimate=pl.CostEstimate(flops=1, bytes_accessed=2 * weight.size, transcendentals=0),
        name="touched",
    )(where, weight)


def whole(value):
    return pl.BlockSpec(value.shape, lambda j, where_ref: (0,) * len(value.shape))


def hidden_terms(name, table, where, tokens, w1, w2):
    half, piece = tokens.shape[1] // 2, w1.shape[1] // NZ
    out = jax.ShapeDtypeStruct((len(table), 2, half, piece), F32)
    block = pl.BlockSpec((2, 2, half, piece), lambda j, where_ref: (j, 0, 0, 0))
    mine, other = call(
        hidden_kernel, name, table, where, [tokens], [whole(tokens)], w1, w2, [out, out], [block, block]
    )
    return mine, other


def joined(t, left, right, left_sib, right_sib):
    mine = jnp.concatenate([left[t], right[t]], axis=1)
    other = jnp.concatenate([left_sib[t], right_sib[t]], axis=1)
    return jnp.concatenate([mine, other], axis=0)


def near_kernel(
    table, where_ref, one_ref, two_ref, one_sib_ref, two_sib_ref, w1_ref, w2_ref, out_ref, w1_buf, w2_buf, sems
):
    step = pl.program_id(0)
    slot = next_pair(step, table, where_ref, w1_ref, w2_ref, w1_buf, w2_buf, sems)

    @pl.when(step == 0)
    def _():
        parts = (one_ref.at[0], one_ref.at[1], one_sib_ref.at[0], one_sib_ref.at[1])
        out_ref[0] = dot(joined(0, *parts), w2_buf[slot])
        out_ref[1] = dot_t(joined(1, *parts), w1_buf[slot])

    @pl.when(step == 1)
    def _():
        parts = (two_ref.at[0], two_ref.at[1], two_sib_ref.at[0], two_sib_ref.at[1])
        out_ref[0] += dot(joined(0, *parts), w2_buf[slot])
        out_ref[1] += dot_t(joined(1, *parts), w1_buf[slot])


def far_kernel(
    table, where_ref, acc_ref, three_ref, three_sib_ref, four_ref, four_sib_ref, own_ref, own_sib_ref, w1_ref, w2_ref,
    out_ref, w1_buf, w2_buf, sems,
):
    step = pl.program_id(0)
    slot = next_pair(step, table, where_ref, w1_ref, w2_ref, w1_buf, w2_buf, sems)

    @pl.when(step == 0)
    def _():
        parts = (three_ref.at[0], three_ref.at[1], three_sib_ref.at[0], three_sib_ref.at[1])
        out_ref[0] = acc_ref[0] + dot(joined(0, *parts), w2_buf[slot])
        out_ref[1] = acc_ref[1] + dot_t(joined(1, *parts), w1_buf[slot])

    @pl.when(step == 1)
    def _():
        parts = (four_ref, own_ref, four_sib_ref, own_sib_ref)
        out_ref[0] += dot(joined(0, *parts), w2_buf[slot])
        out_ref[1] += dot_t(joined(1, *parts), w1_buf[slot])


def summed_over_z(where, tokens, w1, w2):
    mine, other = hidden_terms("first_terms", FIRST, where, tokens, w1, w2)
    sib = to_sibling(other)
    mine2, other2 = hidden_terms("second_terms", SECOND, where, after(tokens, other), w1, w2)
    sib2 = to_sibling(after(other2, sib))

    def total(j):
        if j in FIRST:
            return mine[FIRST.index(j)] + sib[FIRST.index(j)]
        return mine2[SECOND.index(j)] + sib2[SECOND.index(j)]

    quarter = mine.shape[2] // 2
    start = total(4).astype(BF16)
    up, down = along_z(start[:, :quarter], 1).astype(F32), along_z(start[:, quarter:], -1).astype(F32)
    blank = jnp.zeros_like(up)
    up, down = jnp.concatenate([up, blank], axis=1), jnp.concatenate([blank, down], axis=1)
    for far in (3, 2, 1):
        up = along_z((up + total(far)).astype(BF16), 1).astype(F32)
        down = along_z((down + total(NZ - far)).astype(BF16), -1).astype(F32)
    return total(0) + (up + down)


def output_terms(where, own, w1, w2):
    quarter = own.shape[1] // 2
    depth = w1.shape[0]
    ups, downs = [own], [own]
    for _ in range(3):
        ups.append(along_z(ups[-1], 1))
        downs.append(along_z(downs[-1], -1))
    own_sib = to_sibling(own)
    one, two = jnp.stack([ups[1], downs[1]]), jnp.stack([ups[2], downs[2]])
    near = [one, two, to_sibling(one), to_sibling(after(two, (ups[3], downs[3])))]
    three = jnp.stack([ups[3], downs[3]])
    three_sib = to_sibling(three)
    four = along_z(ups[3][:, :quarter], 1), along_z(downs[3][:, quarter:], -1)

    out = jax.ShapeDtypeStruct((2, 2 * own.shape[1], depth), F32)
    specs = [whole(value) for value in near]
    acc = call(near_kernel, "near_terms", NEAR, where, near, specs, w1, w2, out, whole(out))
    four = jnp.concatenate(after(four, acc), axis=1)
    four_sib = to_sibling(four)
    operands = [acc, three, three_sib, four, four_sib, own, own_sib]
    return call(
        far_kernel, "far_terms", FAR, where, operands, [whole(value) for value in operands], w1, w2, out, whole(out),
        input_output_aliases={1: 0},
    )


def per_device(inputs, w1, w2, cotangent):
    row = lax.axis_index("row")
    first = row % 2 == 0
    where = touched(touched((row // 2).astype(jnp.int32).reshape(1), w2), w1)
    block, depth = inputs.shape

    def ordered(by_x, axis):
        low, high = jnp.stack(by_x[:2], axis=axis), jnp.stack(by_x[2:], axis=axis)
        return jnp.where(first, low, high), jnp.where(first, high, low)

    by_x = [inputs] + [along_x(inputs, -r) for r in (1, 2, 3)]
    by_y = [cotangent] + [along_y(cotangent, -k) for k in (1, 2, 3)]
    by_x, by_y = lax.optimization_barrier((by_x, by_y))
    here = jnp.stack(ordered(by_x, 0))
    column = jnp.stack(by_y)
    forward = jnp.stack([here] + [along_y(here, -k) for k in (1, 2, 3)], axis=1)
    backward = jnp.stack(ordered([column] + [along_x(column, -r) for r in (1, 2, 3)], 1))
    tokens = jnp.stack([forward, backward]).reshape(2, NY * NX * block, depth)

    both = summed_over_z(where, tokens, w1, w2)
    out = output_terms(where, jnp.stack(gelu_both(both[0], both[1])), w1, w2)
    out = out.reshape(2, 2, NY, 2, block, depth)

    def by_distance(halves, axis):
        low, high = jnp.where(first, halves[0], halves[1]), jnp.where(first, halves[1], halves[0])
        return [lax.index_in_dim(part, r, axis, keepdims=False) for part in (low, high) for r in range(2)]

    def summed(parts, along, kind):
        total = parts[0]
        for distance in (2, 1, 3):
            total = total + along(parts[distance].astype(kind), distance).astype(F32)
        return total

    forward = summed([out[0, :, k] for k in range(NY)], along_y, BF16)
    backward = summed(by_distance(out[1], 1), along_x, BF16)
    forward = summed(by_distance(forward, 0), along_x, F32)
    backward = summed([backward[k] for k in range(NY)], along_y, F32)
    return forward.astype(BF16), backward.astype(BF16)


def solution(mesh):
    return jax.shard_map(
        per_device,
        mesh=mesh,
        in_specs=(P("col", "row"), P("row", "col"), P("col", "row"), P("col", "row")),
        out_specs=(P("col", "row"), P("col", "row")),
        check_vma=False,
    )
```

```python
import functools

import jax
import jax.numpy as jnp
from jax import lax
from jax.experimental import pallas as pl
from jax.experimental.pallas import tpu as pltpu
from jax.sharding import PartitionSpec as P

NZ, NY, NX = 8, 4, 4
BF16, F32 = jnp.bfloat16, jnp.float32
VMEM_LIMIT = 20 * 2**20
LIGHT = pl.CostEstimate(flops=1, bytes_accessed=1, transcendentals=0)
HEAVY = pl.CostEstimate(flops=4 * 512 * 768 * 5 * 384, bytes_accessed=5 * 2**22, transcendentals=0)


def along_z(value, step):
    moves = [(2 * z + c, 2 * ((z + step) % NZ) + c) for z in range(NZ) for c in range(2)]
    return lax.ppermute(value, "row", moves)


def along_x(value, step):
    moves = [(NX * y + x, NX * y + (x + step) % NX) for y in range(NY) for x in range(NX)]
    return lax.ppermute(value, "col", moves)


def along_y(value, step):
    moves = [(NX * y + x, NX * ((y + step) % NY) + x) for y in range(NY) for x in range(NX)]
    return lax.ppermute(value, "col", moves)


def to_sibling(value):
    return lax.ppermute(value, "row", [(i, i ^ 1) for i in range(2 * NZ)])


def after(value, earlier):
    return lax.optimization_barrier((value, earlier))[0]


def gelu_both(pre_act, grad_act):
    factor = 0.7978845608028654
    tangent = jnp.tanh(factor * (pre_act + 0.044715 * pre_act * pre_act * pre_act))
    activated = (0.5 * pre_act * (1.0 + tangent)).astype(BF16)
    derivative = 0.5 * (1.0 + tangent) + 0.5 * pre_act * (1.0 - tangent * tangent) * factor * (
        1.0 + 3.0 * 0.044715 * pre_act * pre_act
    )
    return activated, (grad_act * derivative).astype(BF16)


def dot(left, right):
    return jnp.dot(left, right, preferred_element_type=F32)


def dot_t(left, right):
    return lax.dot_general(left, right, (((1,), (1,)), ((), ())), preferred_element_type=F32)


FIRST, SECOND = (4, 3), (5, 2, 6, 1, 7, 0)
NEAR, FAR = (7, 1, 6, 2), (5, 3, 4, 0)


def pick(step, table):
    value = jnp.int32(table[0])
    for place, entry in enumerate(table):
        value = jnp.where(step == place, entry, value)
    return value


def next_pair(step, table, where_ref, w1_ref, w2_ref, w1_buf, w2_buf, sems):
    piece = w1_buf.shape[2] // 2

    def copies(at, slot, part):
        place = pl.ds(pl.multiple_of(at * piece, piece), piece)
        half = pl.ds(part * piece, piece)
        return (
            pltpu.make_async_copy(w1_ref.at[:, place], w1_buf.at[slot, :, half], sems.at[part, slot]),
            pltpu.make_async_copy(w2_ref.at[place, :], w2_buf.at[slot, half, :], sems.at[2 + part, slot]),
        )

    def start(pair):
        for part in range(2):
            at = lax.rem(where_ref[0] + pick(pair, table[part::2]), NZ)
            for copy in copies(at, lax.rem(pair, 3), part):
                copy.start()

    @pl.when(step == 0)
    def _():
        start(jnp.int32(0))
        if len(table) > 2:
            start(jnp.int32(1))

    @pl.when(step + 2 < len(table) // 2)
    def _():
        start(step + 2)

    slot = lax.rem(step, 3)
    for part in range(2):
        for copy in copies(0, slot, part):
            copy.wait()
    return slot


def weight_buffers(depth, piece):
    return [
        pltpu.VMEM((3, depth, 2 * piece), BF16),
        pltpu.VMEM((3, 2 * piece, depth), BF16),
        pltpu.SemaphoreType.DMA((4, 3)),
    ]


def hidden_kernel(table, where_ref, x_ref, w1_ref, w2_ref, mine_ref, other_ref, w1_buf, w2_buf, sems):
    slot = next_pair(pl.program_id(0), table, where_ref, w1_ref, w2_ref, w1_buf, w2_buf, sems)
    half, piece = mine_ref.shape[2:]
    for t, terms in enumerate((lambda: dot(x_ref[0], w1_buf[slot]), lambda: dot_t(x_ref[1], w2_buf[slot]))):
        value = terms()
        for part in range(2):
            columns = slice(part * piece, (part + 1) * piece)
            mine_ref[part, t] = value[:half, columns]
            other_ref[part, t] = value[half:, columns]


def call(kernel, name, table, where, operands, specs, w1, w2, out_shape, out_specs, **more):
    depth, piece = w1.shape[0], w1.shape[1] // NZ
    return pl.pallas_call(
        functools.partial(kernel, table),
        grid_spec=pltpu.PrefetchScalarGridSpec(
            num_scalar_prefetch=1,
            grid=(len(table) // 2,),
            in_specs=specs + [pl.BlockSpec(memory_space=pl.ANY)] * 2,
            out_specs=out_specs,
            scratch_shapes=weight_buffers(depth, piece),
        ),
        out_shape=out_shape,
        cost_estimate=HEAVY if name in ("second_terms", "far_forward") else LIGHT,
        compiler_params=pltpu.CompilerParams(vmem_limit_bytes=VMEM_LIMIT),
        name=name,
        **more,
    )(where, *operands, w1, w2)


def touch_kernel(where_ref, weight_ref, out_ref):
    out_ref[0] = where_ref[0]


def touched(where, weight):
    return pl.pallas_call(
        touch_kernel,
        in_specs=[pl.BlockSpec(memory_space=pltpu.SMEM), pl.BlockSpec(memory_space=pl.ANY)],
        out_specs=pl.BlockSpec(memory_space=pltpu.SMEM),
        out_shape=jax.ShapeDtypeStruct((1,), jnp.int32),
        cost_estimate=pl.CostEstimate(flops=1, bytes_accessed=2 * weight.size, transcendentals=0),
        name="touched",
    )(where, weight)


def whole(value):
    return pl.BlockSpec(value.shape, lambda j, where_ref: (0,) * len(value.shape))


def hidden_terms(name, table, where, tokens, w1, w2):
    half, piece = tokens.shape[1] // 2, w1.shape[1] // NZ
    out = jax.ShapeDtypeStruct((len(table), 2, half, piece), F32)
    block = pl.BlockSpec((2, 2, half, piece), lambda j, where_ref: (j, 0, 0, 0))
    mine, other = call(
        hidden_kernel, name, table, where, [tokens], [whole(tokens)], w1, w2, [out, out], [block, block]
    )
    return mine, other


def joined(t, left, right, left_sib, right_sib):
    mine = jnp.concatenate([left[t], right[t]], axis=1)
    other = jnp.concatenate([left_sib[t], right_sib[t]], axis=1)
    return jnp.concatenate([mine, other], axis=0)


def near_kernel(
    table, where_ref, one_ref, two_ref, one_sib_ref, two_sib_ref, w1_ref, w2_ref, out_ref, w1_buf, w2_buf, sems
):
    step = pl.program_id(0)
    slot = next_pair(step, table, where_ref, w1_ref, w2_ref, w1_buf, w2_buf, sems)

    @pl.when(step == 0)
    def _():
        parts = (one_ref.at[0], one_ref.at[1], one_sib_ref.at[0], one_sib_ref.at[1])
        out_ref[0] = dot(joined(0, *parts), w2_buf[slot])
        out_ref[1] = dot_t(joined(1, *parts), w1_buf[slot])

    @pl.when(step == 1)
    def _():
        parts = (two_ref.at[0], two_ref.at[1], two_sib_ref.at[0], two_sib_ref.at[1])
        out_ref[0] += dot(joined(0, *parts), w2_buf[slot])
        out_ref[1] += dot_t(joined(1, *parts), w1_buf[slot])


def far_kernel(
    t, table, where_ref, acc_ref, three_ref, three_sib_ref, four_ref, four_sib_ref, own_ref, own_sib_ref, w1_ref, w2_ref,
    out_ref, w1_buf, w2_buf, sems,
):
    step = pl.program_id(0)
    slot = next_pair(step, table, where_ref, w1_ref, w2_ref, w1_buf, w2_buf, sems)

    def product(*parts):
        rows = joined(0, *parts)
        return dot(rows, w2_buf[slot]) if t == 0 else dot_t(rows, w1_buf[slot])

    @pl.when(step == 0)
    def _():
        parts = (three_ref.at[0], three_ref.at[1], three_sib_ref.at[0], three_sib_ref.at[1])
        out_ref[...] = acc_ref[0] + product(*parts)

    @pl.when(step == 1)
    def _():
        out_ref[...] += product(four_ref, own_ref, four_sib_ref, own_sib_ref)


def summed_over_z(where, tokens, w1, w2):
    mine, other = hidden_terms("first_terms", FIRST, where, tokens, w1, w2)
    sib = to_sibling(other)
    mine2, other2 = hidden_terms("second_terms", SECOND, where, after(tokens, other), w1, w2)
    sib2 = to_sibling(after(other2, sib))

    def total(j):
        if j in FIRST:
            return mine[FIRST.index(j)] + sib[FIRST.index(j)]
        return mine2[SECOND.index(j)] + sib2[SECOND.index(j)]

    quarter = mine.shape[2] // 2
    start = total(4).astype(BF16)
    up, down = along_z(start[:, :quarter], 1).astype(F32), along_z(start[:, quarter:], -1).astype(F32)
    blank = jnp.zeros_like(up)
    up, down = jnp.concatenate([up, blank], axis=1), jnp.concatenate([blank, down], axis=1)
    for far in (3, 2, 1):
        up = along_z((up + total(far)).astype(BF16), 1).astype(F32)
        down = along_z((down + total(NZ - far)).astype(BF16), -1).astype(F32)
    return total(0) + (up + down)


def output_terms(where, own, w1, w2):
    quarter = own.shape[1] // 2
    depth = w1.shape[0]
    ups, downs = [own], [own]
    for _ in range(3):
        ups.append(along_z(ups[-1], 1))
        downs.append(along_z(downs[-1], -1))
    own_sib = to_sibling(own)
    one, two = jnp.stack([ups[1], downs[1]]), jnp.stack([ups[2], downs[2]])
    near = [one, two, to_sibling(one), to_sibling(after(two, (ups[3], downs[3])))]
    three = jnp.stack([ups[3], downs[3]])
    three_sib = to_sibling(three)
    four = along_z(ups[3][:, :quarter], 1), along_z(downs[3][:, quarter:], -1)

    out = jax.ShapeDtypeStruct((2, 2 * own.shape[1], depth), F32)
    specs = [whole(value) for value in near]
    acc = call(near_kernel, "near_terms", NEAR, where, near, specs, w1, w2, out, whole(out))
    four = jnp.concatenate(after(four, acc), axis=1)
    four_sib = to_sibling(four)
    operands = [acc, three, three_sib, four, four_sib, own, own_sib]
    out = jax.ShapeDtypeStruct(acc.shape[1:], F32)

    def of(t, value):
        if value.ndim == 4:
            return pl.BlockSpec((2, 1, *value.shape[2:]), lambda j, where_ref: (0, t, 0, 0))
        return pl.BlockSpec((1, *value.shape[1:]), lambda j, where_ref: (t, 0, 0))

    def far(t, name, here):
        specs = [of(t, value) for value in operands]
        return call(functools.partial(far_kernel, t), name, FAR, here, operands, specs, w1, w2, out, whole(out))

    backward = far(1, "far_backward", where)
    return far(0, "far_forward", after(where, backward)), backward


def per_device(inputs, w1, w2, cotangent):
    row = lax.axis_index("row")
    first = row % 2 == 0
    where = touched(touched((row // 2).astype(jnp.int32).reshape(1), w2), w1)
    block, depth = inputs.shape

    def ordered(by_x, axis):
        low, high = jnp.stack(by_x[:2], axis=axis), jnp.stack(by_x[2:], axis=axis)
        return jnp.where(first, low, high), jnp.where(first, high, low)

    by_x = [inputs] + [along_x(inputs, -r) for r in (1, 2, 3)]
    by_y = [cotangent] + [along_y(cotangent, -k) for k in (1, 2, 3)]
    by_x, by_y = lax.optimization_barrier((by_x, by_y))
    here = jnp.stack(ordered(by_x, 0))
    column = jnp.stack(by_y)
    forward = jnp.stack([here] + [along_y(here, -k) for k in (1, 2, 3)], axis=1)
    backward = jnp.stack(ordered([column] + [along_x(column, -r) for r in (1, 2, 3)], 1))
    tokens = jnp.stack([forward, backward]).reshape(2, NY * NX * block, depth)

    both = summed_over_z(where, tokens, w1, w2)
    out = output_terms(where, jnp.stack(gelu_both(both[0], both[1])), w1, w2)
    out = [value.reshape(2, NY, 2, block, depth) for value in out]

    def by_distance(halves, axis):
        low, high = jnp.where(first, halves[0], halves[1]), jnp.where(first, halves[1], halves[0])
        return [lax.index_in_dim(part, r, axis, keepdims=False) for part in (low, high) for r in range(2)]

    def summed(parts, along, kind):
        total = parts[0]
        for distance in (2, 1, 3):
            total = total + along(parts[distance].astype(kind), distance).astype(F32)
        return total

    forward = summed([out[0][:, k] for k in range(NY)], along_y, BF16)
    backward = summed(by_distance(out[1], 1), along_x, BF16)
    forward = summed(by_distance(forward, 0), along_x, F32)
    backward = summed([backward[k] for k in range(NY)], along_y, F32)
    return forward.astype(BF16), backward.astype(BF16)


def solution(mesh):
    return jax.shard_map(
        per_device,
        mesh=mesh,
        in_specs=(P("col", "row"), P("row", "col"), P("col", "row"), P("col", "row")),
        out_specs=(P("col", "row"), P("col", "row")),
        check_vma=False,
    )
```
